32 devices in a mesh: grp: 2 (over y), ka: 4 (over z), pb: 4 (over x, core).
Axes of the slice: x: 2, y: 2, z: 4, core: 2. Of those that a mesh axis runs over, the one named last changes fastest.
Arguments:
- kpoint_coords: float32 [3, 128], P(None, ('grp', 'ka')), parts along dimension 1, may hold values from 0 to 1
- g_wannier: bfloat16 [8, 8, 192000], P(('grp', 'pb'), None, 'ka'), parts along dimension 0, may hold values from -0.0234375 to 0.0234375
- mode_vectors: bfloat16 [8, 2, 60, 60], P(('grp', 'pb')), parts along dimension 0, may hold values from -0.5 to 0.5
- frequencies: float32 [8, 60], P(('grp', 'pb')), parts along dimension 0, may hold values from 0.02 to 0.2
- rotations: bfloat16 [128, 3200], P(('grp', 'ka')), parts along dimension 0, may hold values from -0.625 to 0.625
- energies: bfloat16 [128, 40], P(('grp', 'ka')), parts along dimension 0, may hold values from -0.29882812 to 0.29882812
- band_window: int32 [2, 128], P(None, ('grp', 'ka')), parts along dimension 1, may hold values from 0 to 40, as said below
- target_owner: int32 [8, 64, 1], P(('grp', 'pb'), 'ka'), parts along dimension 0, may hold values from 0 to 3; in each aligned block of 16 rows (0 to 15, 16 to 31, ..., all dimensions but the last counted through in order) at most 8 rows name the same one
- target_row: int32 [8, 64], P(('grp', 'pb'), 'ka'), parts along dimension 0, may hold values from 0 to 15
Outputs:
- electron_width: float32 [128, 40], P(('grp', 'ka')), parts along dimension 0
- phonon_width: float32 [8, 60], P(('grp', 'pb')), parts along dimension 0
The draws below stay inside these ranges and needn't reach their ends.
There are 2 independent parts, one for each index of `grp`. The reference program is written for one: setup_inputs(seed, part) draws one part's arguments, and reference() takes and returns one part's arrays. A program takes and returns all parts, laid end to end along the dimension named above; each array names one. Nothing has to cross between parts.
Inputs may be any that keep to these rules, and one draw needn't show every extreme that they name: `target_owner`: among the 16 pairs of one device (one q point, one block of k points), no owner index is named more than 8 times; in every draw some device's pairs name one owner exactly 8 times. `band_window`: row 0 is the first band of a k point's window and row 1 one past its last; every window holds at least half of the bands, and some k point's window holds all of them.
All inputs are finite; a program needn't handle non-finite values.
Results may differ from the reference program's by a relative error of at most 0.0014.
Values may be sent and summed in bfloat16 or wider, within the bound.
A program may use at most 256 MiB of HBM per device.

```python
import math
import jax
import jax.numpy as jnp
import numpy as np
from jax import lax

BANDS = 40
MODES = 60
R_E = 8
K_DEV = 16
NK = 64
NQ = 4
CAP = 8
N_KA = 4


def draw_band_window(key, part):
    key = jax.random.fold_in(key, 7)
    first_key, second_key = jax.random.split(key)
    lowest = jax.random.randint(first_key, (NK,), 0, BANDS // 4 + 1)
    highest = jax.random.randint(second_key, (NK,), 3 * BANDS // 4, BANDS + 1)
    lowest = lowest.at[0].set(0)
    highest = highest.at[0].set(BANDS)
    return jnp.stack([lowest, highest]).astype(jnp.int32)


def touch_ends(entries, own_key, least, top_value):
    longest = entries.shape.index(max(entries.shape))
    spots = []
    for shift in (0, 1):
        where = [jax.random.randint(jax.random.fold_in(own_key, axis), (), 0, length) for axis, length in enumerate(entries.shape)]
        where[longest] = (where[longest] + shift) % entries.shape[longest]
        spots.append(tuple(where))
    return entries.at[spots[0]].set(least).at[spots[1]].set(top_value)


def block_levels(rng, shape, cuts, smallest, top_value):
    gain = 1.0
    for dim, shards_of in cuts:
        heights = jax.random.uniform(jax.random.fold_in(jax.random.fold_in(rng, 6), dim), (shards_of,), jnp.float32, smallest / len(cuts), top_value / len(cuts))
        gain = gain * jnp.repeat(jnp.exp(heights), shape[dim] // shards_of).reshape((-1,) + (1,) * (len(shape) - 1 - dim))
    return gain


def assign_block(key, own, number, rows, amount, top, bound, slope):
    ranking = jax.random.permutation(key, amount)
    packed, ordinary = portions_of(amount, rows * top, bound, slope, True), portions_of(amount, rows * top, bound, slope, False)
    places = jnp.arange(amount)

    def named(lengths, turn):
        used = int((lengths > 0).sum())
        fixed = max(1, used // 4)
        moved = fixed + (places - fixed + turn * (used - fixed)) % max(1, amount - fixed)
        return jnp.zeros((amount,), jnp.int32).at[ranking[jnp.where(places < fixed, places, moved)]].set(jnp.asarray(lengths, jnp.int32))

    lengths = jnp.where(number % 4 == 0, named(packed, number // 4), named(ordinary, number - number // 4 - 1))
    mixed = jax.random.permutation(jax.random.fold_in(own, 3), amount)
    donor, receiver = mixed[0:amount // 2 * 2:2], mixed[1:amount // 2 * 2:2]
    slack = jnp.minimum(lengths[donor] - 1, bound - lengths[receiver]) // 2
    slack = jnp.where((donor == ranking[0]) | (receiver == ranking[0]) | (lengths[receiver] == 0), 0, jnp.maximum(slack, 0))
    moved = jax.random.randint(jax.random.fold_in(own, 4), (amount // 2,), 0, 1 << 20) % (slack + 1)
    lengths = lengths.at[donor].add(-moved).at[receiver].add(moved)
    labels = jnp.searchsorted(jnp.cumsum(lengths), jnp.arange(rows * top), side="right").astype(jnp.int32)
    table = labels.reshape(top, rows).T
    table = table[jax.random.permutation(jax.random.fold_in(own, 1), rows)]
    turn = jax.random.randint(jax.random.fold_in(own, 2), (rows, 1), 0, top)
    return jnp.take_along_axis(table, (jnp.arange(top)[None, :] + turn) % top, axis=1)


def portions_of(count, total, limit, slope, full):
    weights = [(1 << 20) // math.isqrt(rank ** slope) + 1 for rank in range(1, count + 1)]
    largest = limit if full else min(limit, max(-(-total // count), total * weights[0] // sum(weights)))
    least = 1 if total - largest >= count - 1 else 0
    given, surplus = [largest] + [least] * (count - 1), total - largest - least * (count - 1)
    while surplus > 0:
        free = [i for i in range(1, count) if given[i] < largest] or [i for i in range(1, count) if given[i] < limit]
        pool, left = sum([weights[i] for i in free]), surplus
        for i in free:
            extra = min(limit - given[i], max(1, left * weights[i] // pool), surplus)
            given[i] = given[i] + extra
            surplus = surplus - extra
    return np.array(given)


def scatter_about(rng, extent, deviation, limit, pieces=(), kind=jnp.bfloat16):
    factor_of = block_levels(rng, extent, pieces, -0.22, 0.18) if pieces else 1.0
    values = jax.random.normal(rng, extent, jnp.float32) * deviation * factor_of
    return jnp.minimum(jnp.maximum(values, -limit), limit).astype(kind)


def setup_inputs(seed: int = 0, part: int = 0) -> dict:
    key_list = jax.random.split(jax.random.key(seed), 10)
    part_splits = jax.random.split(jax.random.fold_in(key_list[9], part), 10)
    kpoint_coords = jnp.clip(1.0 * jax.random.uniform(part_splits[0], (3, NK), jnp.float32) ** block_levels(part_splits[0], (3, NK), ((1, 4),), -0.2, 0.2), 0.0, 1.0)
    g_wannier = scatter_about(part_splits[1], (NQ, R_E, 2 * MODES * BANDS * BANDS), (4 * R_E * MODES * BANDS) ** -0.5, 0.0234375, ((0, 4), (2, 4)))
    mode_vectors = scatter_about(part_splits[2], (NQ, 2, MODES, MODES), (2 * MODES) ** -0.5, 0.5, ((0, 4),))
    frequencies = jnp.clip(jnp.exp(math.log(0.2) - 2.3025851 * jax.random.uniform(part_splits[3], (NQ, MODES), jnp.float32) ** block_levels(part_splits[3], (NQ, MODES), ((0, 4),), -0.2, 0.2)), 0.02, 0.2)
    rotations = scatter_about(part_splits[4], (NK, 2 * BANDS * BANDS), (2 * BANDS) ** -0.5, 0.625, ((0, 4),))
    energies = jnp.clip(jax.random.uniform(part_splits[5], (NK, BANDS), jnp.float32, -0.29882812, 0.29882812) * block_levels(part_splits[5], (NK, BANDS), ((0, 4),), -0.4, 0.0), -0.29882812, 0.29882812).astype(jnp.bfloat16)
    band_window = draw_band_window(jax.random.fold_in(jax.random.fold_in(key_list[9], part), 71), part)
    target_owner_keys = jax.random.split(jax.random.fold_in(part_splits[7], 1), NQ * NK // K_DEV)
    target_owner_turns = jax.random.permutation(jax.random.fold_in(part_splits[7], 3), NQ * NK // K_DEV)
    target_owner = jax.vmap(lambda own, number: assign_block(jax.random.fold_in(part_splits[7], 2), own, number, K_DEV, N_KA, 1, CAP, 2))(target_owner_keys, target_owner_turns).reshape((NQ, NK, 1))
    target_row = touch_ends(jax.random.randint(part_splits[8], (NQ, NK), 0, K_DEV), jax.random.fold_in(part_splits[8], 1), 0, K_DEV - 1).astype(jnp.int32)
    return dict(kpoint_coords=kpoint_coords, g_wannier=g_wannier, mode_vectors=mode_vectors, frequencies=frequencies, rotations=rotations, energies=energies, band_window=band_window, target_owner=target_owner, target_row=target_row)


THERMAL_KELVIN = 0.1
SMEARING_WIDTH = 0.05


def window_mask(band_window, bands):
    energy_levels = jnp.arange(bands, dtype=jnp.int32)
    inside = (energy_levels[None, :] >= band_window[0][:, None]) & (energy_levels[None, :] < band_window[1][:, None])
    return inside.astype(jnp.float32)


def phases_of(coords, vectors):
    index = jnp.arange(vectors, dtype=jnp.int32)
    first = (index % 2).astype(jnp.float32)
    second = ((index // 2) % 2).astype(jnp.float32)
    third = ((index // 4) % 2).astype(jnp.float32)
    angle = coords[0][:, None] * first[None, :] + coords[1][:, None] * second[None, :]
    angle = 2.0 * math.pi * (angle + coords[2][:, None] * third[None, :])
    return jnp.concatenate([jnp.cos(angle), jnp.sin(angle)], 0).astype(jnp.bfloat16)


def lorentz(value):
    return (SMEARING_WIDTH / math.pi) / (value * value + SMEARING_WIDTH * SMEARING_WIDTH)


def occupation(energy_value):
    return 1.0 / (1.0 + jnp.exp(energy_value / THERMAL_KELVIN))


def pair_terms(fourier_sum, mode_pair, phonon_frequency, rot_here, eps_here, mask_here, rot_there, eps_there, mask_there, count_q, count_k):
    real_part = fourier_sum[0, :, 0] - fourier_sum[1, :, 1]
    imag_part = fourier_sum[1, :, 0] + fourier_sum[0, :, 1]
    wannier = jnp.stack([real_part, imag_part]).astype(jnp.bfloat16)
    mode_re = mode_pair[0]
    mode_im = mode_pair[1]
    mode_block = jnp.stack([jnp.stack([mode_re, mode_im], -1), jnp.stack([-mode_im, mode_re], -1)])
    modal = jnp.einsum('ckmab,cmvd->dkvab', wannier.astype(jnp.float32), mode_block.astype(jnp.float32)).astype(jnp.bfloat16)
    right_re = rot_here[:, 0]
    right_im = rot_here[:, 1]
    right = jnp.stack([jnp.stack([right_re, right_im], -1), jnp.stack([-right_im, right_re], -1)], 1)
    half = jnp.einsum('ckvab,kcbnd->dkvan', modal.astype(jnp.float32), right.astype(jnp.float32)).astype(jnp.bfloat16)
    left_re = rot_there[:, 0]
    left_im = rot_there[:, 1]
    left = jnp.stack([jnp.stack([left_re, -left_im], -1), jnp.stack([left_im, left_re], -1)], 1)
    coupling = jnp.einsum('ckvan,kcamd->dkvmn', half.astype(jnp.float32), left.astype(jnp.float32))
    strength = coupling[0] * coupling[0] + coupling[1] * coupling[1]
    e_here = eps_here.astype(jnp.float32)
    e_there = eps_there.astype(jnp.float32)
    gap = e_here[:, None, :] - e_there[:, :, None]
    bose_einstein_factor = 1.0 / (jnp.exp(phonon_frequency / THERMAL_KELVIN) - 1.0)
    occ_here = occupation(e_here)
    occ_there = occupation(e_there)
    shifted = phonon_frequency[None, :, None, None]
    upward = lorentz(gap[:, None] + shifted)
    descending_transition = lorentz(gap[:, None] - shifted)
    bose_wide = bose_einstein_factor[None, :, None, None]
    occ_wide = occ_there[:, None, :, None]
    emission = (bose_wide + occ_wide) * upward + (bose_wide + 1.0 - occ_wide) * descending_transition
    weighted = strength * (mask_here[:, None, :] * mask_there[:, :, None])[:, None]
    self_part = jnp.sum(weighted * emission, axis=(1, 2)) / count_q
    change = occ_here[:, None, None, :] - occ_wide
    width_part = (2.0 * math.pi / count_k) * jnp.sum(weighted * change * upward, axis=(0, 2, 3))
    return self_part, width_part


def reference(kpoint_coords, g_wannier, mode_vectors, frequencies, rotations, energies, band_window, target_owner, target_row):
    band_mask = window_mask(band_window, BANDS)
    target = (target_owner[:, :, 0] * K_DEV + target_row).astype(jnp.int32)
    blocks = NK // K_DEV

    def per_q(q_index):
        coupling_q = lax.dynamic_index_in_dim(g_wannier, q_index, 0, False)
        modes_q = lax.dynamic_index_in_dim(mode_vectors, q_index, 0, False)
        freq_q = lax.dynamic_index_in_dim(frequencies, q_index, 0, False)
        target_q = lax.dynamic_index_in_dim(target, q_index, 0, False)

        def per_block(block):
            offset = (block * K_DEV).astype(jnp.int32)
            coords = lax.dynamic_slice_in_dim(kpoint_coords, offset, K_DEV, 1)
            phases = phases_of(coords, R_E)
            fourier_sum = jnp.dot(phases, coupling_q, preferred_element_type=jnp.float32)
            fourier_sum = fourier_sum.reshape(2, K_DEV, 2, MODES, BANDS, BANDS)
            rot_here = lax.dynamic_slice_in_dim(rotations, offset, K_DEV, 0).reshape(K_DEV, 2, BANDS, BANDS)
            eps_here = lax.dynamic_slice_in_dim(energies, offset, K_DEV, 0)
            mask_here = lax.dynamic_slice_in_dim(band_mask, offset, K_DEV, 0)
            wanted = lax.dynamic_slice_in_dim(target_q, offset, K_DEV, 0)
            rot_there = jnp.take(rotations, wanted, axis=0).reshape(K_DEV, 2, BANDS, BANDS)
            eps_there = jnp.take(energies, wanted, axis=0)
            mask_there = jnp.take(band_mask, wanted, axis=0)
            return pair_terms(fourier_sum, modes_q, freq_q, rot_here, eps_here, mask_here, rot_there, eps_there, mask_there, NQ, NK)

        self_part, width_part = lax.map(per_block, jnp.arange(blocks, dtype=jnp.int32))
        return self_part.reshape(NK, BANDS), jnp.sum(width_part, 0)

    self_all, width_all = lax.map(per_q, jnp.arange(NQ, dtype=jnp.int32))
    return jnp.sum(self_all, 0), width_all
```

```python
import functools
import math

import jax
import jax.numpy as jnp
from jax import lax
from jax.experimental import pallas as pl
from jax.experimental.pallas import tpu as pltpu
from jax.sharding import PartitionSpec as P

THERMAL_KELVIN = 0.1
SMEARING_WIDTH = 0.05
LANES = 128
HALF = 64


def window_mask(band_window, bands):
    energy_levels = jnp.arange(bands, dtype=jnp.int32)
    inside = (energy_levels[None, :] >= band_window[0][:, None]) & (
        energy_levels[None, :] < band_window[1][:, None]
    )
    return inside.astype(jnp.float32)


def phases_of(coords, vectors):
    index = jnp.arange(vectors, dtype=jnp.int32)
    first = (index % 2).astype(jnp.float32)
    second = (index // 2 % 2).astype(jnp.float32)
    third = (index // 4 % 2).astype(jnp.float32)
    angle = coords[0][:, None] * first[None, :] + coords[1][:, None] * second[None, :]
    angle = 2.0 * math.pi * (angle + coords[2][:, None] * third[None, :])
    return jnp.concatenate([jnp.cos(angle), jnp.sin(angle)], 0).astype(jnp.bfloat16)


def occupation(energy_value):
    return 1.0 / (1.0 + jnp.exp(energy_value / THERMAL_KELVIN))


def pair_kernel(
    g_ref, w_ref, right_ref, left_ref, e_ref, up_ref, mask_ref, shift_ref, gain_ref, occ_ref, keep_ref,
    self_ref, width_ref, turned, modal, half, *, modes, bands
):
    area = bands * bands
    vectors = g_ref.shape[0]
    blocks = 2 * area // LANES
    per = LANES // vectors
    step = pl.program_id(0)

    @pl.when(step == 0)
    def _():
        width_ref[...] = jnp.zeros_like(width_ref)

        def turn(j, carry):
            for group in range(turned.shape[1] // LANES):
                rows = []
                for p in range(group * per, group * per + per):
                    if p < modes:
                        at = pl.multiple_of(p * 2 * area + j * LANES, LANES)
                        rows.append(g_ref[:, pl.ds(at, LANES)].astype(jnp.float32))
                    else:
                        rows.append(jnp.zeros((vectors, LANES), jnp.float32))
                tile = jnp.concatenate(rows, 0).T
                spot = pl.ds(pl.multiple_of(j * LANES, LANES), LANES)
                turned[spot, group * LANES : (group + 1) * LANES] = tile.astype(jnp.bfloat16)
            return carry

        lax.fori_loop(0, blocks, turn, 0)

    chunk = 8 * bands

    for c in range(area // chunk):
        first = c * chunk
        both = jnp.dot(turned[first : first + chunk, :], w_ref[0], preferred_element_type=jnp.float32)
        both += jnp.dot(
            turned[area + first : area + first + chunk, :], w_ref[1], preferred_element_type=jnp.float32
        )
        for kk in range(2):
            modal[kk, first : first + chunk, :] = both[:, kk * LANES : (kk + 1) * LANES]

    lane = lax.broadcasted_iota(jnp.int32, (bands, LANES), 1)
    sign = jnp.where(lane < HALF, -1.0, 1.0)

    def operand(block):
        block = jnp.concatenate([block, pltpu.roll(block, HALF, 1) * sign], 0)
        return block.astype(jnp.bfloat16)

    def one_k(kk, carry):
        k = step * 2 + kk
        right = right_ref[kk]
        for a in range(0, bands, 2):
            pair = [operand(modal[kk, (a + s) * bands : (a + s + 1) * bands, :]) for s in range(2)]
            out = jnp.dot(right, jnp.concatenate(pair, 1), preferred_element_type=jnp.float32)
            for s in range(2):
                half[pl.ds(a + s, bands, stride=bands), :] = out[:, s * LANES : (s + 1) * LANES]
        left = left_ref[kk]
        shift = shift_ref[kk]
        gain = gain_ref[kk]
        occ = occ_ref[kk]
        total = jnp.zeros((bands, LANES), jnp.float32)
        for n in range(0, bands, 2):
            pair = [operand(half[(n + s) * bands : (n + s + 1) * bands, :]) for s in range(2)]
            out = jnp.dot(left, jnp.concatenate(pair, 1), preferred_element_type=jnp.float32)
            for s in range(2):
                coupling = out[:, s * LANES : (s + 1) * LANES]
                square = coupling * coupling
                strength = square + pltpu.roll(square, HALF, 1)
                x = shift + e_ref[k, n + s]
                term = strength / (x * x + SMEARING_WIDTH * SMEARING_WIDTH)
                self_ref[kk, n + s : n + s + 1, :] = jnp.sum(term * gain, 0, keepdims=True)
                total += term * (up_ref[k, n + s] - mask_ref[k, n + s] * occ)
        width_ref[...] += total * keep_ref[kk]
        return carry

    lax.fori_loop(0, 2, one_k, 0)


def pair_sums(g, weights, right, left, e_here, up_here, mask_here, shift, gain, occ, keep, modes, bands):
    local_k = right.shape[0]
    depth = weights.shape[1]
    area = bands * bands
    by_k = lambda i: (i, 0, 0)
    table = pl.BlockSpec((2, bands, LANES), by_k)
    return pl.pallas_call(
        functools.partial(pair_kernel, modes=modes, bands=bands),
        grid=(local_k // 2,),
        in_specs=[
            pl.BlockSpec(g.shape, lambda i: (0, 0)),
            pl.BlockSpec((2, depth, 2 * LANES), lambda i: (0, 0, i)),
            pl.BlockSpec((2,) + right.shape[1:], by_k),
            pl.BlockSpec((2,) + left.shape[1:], by_k),
            pl.BlockSpec(memory_space=pltpu.SMEM),
            pl.BlockSpec(memory_space=pltpu.SMEM),
            pl.BlockSpec(memory_space=pltpu.SMEM),
            table,
            table,
            table,
            table,
        ],
        out_specs=[table, pl.BlockSpec((bands, LANES), lambda i: (0, 0))],
        out_shape=[
            jax.ShapeDtypeStruct((local_k, bands, LANES), jnp.float32),
            jax.ShapeDtypeStruct((bands, LANES), jnp.float32),
        ],
        scratch_shapes=[
            pltpu.VMEM((2 * area, depth), jnp.bfloat16),
            pltpu.VMEM((2, area, LANES), jnp.float32),
            pltpu.VMEM((area, LANES), jnp.float32),
        ],
        compiler_params=pltpu.CompilerParams(vmem_limit_bytes=48 * 1024 * 1024),
        name="pairs",
    )(g, weights, right, left, e_here, up_here, mask_here, shift, gain, occ, keep)


def lanes_of(first, second):
    pad = [(0, 0)] * (first.ndim - 1) + [(0, HALF - first.shape[-1])]
    return jnp.concatenate([jnp.pad(first, pad), jnp.pad(second, pad)], -1)


def weights_of(phases, mode_pair):
    _, local_k, vectors = phases.shape
    modes = mode_pair.shape[1]
    wave = phases.astype(jnp.float32)
    vec = mode_pair.astype(jnp.float32).reshape(2, modes // 2, 2, modes)
    vec = jnp.transpose(vec, (0, 2, 1, 3))[:, :, :, None, None, :]
    cos, sin = (jnp.transpose(w)[None, None, :, :, None] for w in (wave[0], wave[1]))
    real = cos * vec[0] - sin * vec[1]
    imag = cos * vec[1] + sin * vec[0]
    both = jnp.stack([lanes_of(real, imag), lanes_of(-imag, real)], 1).astype(jnp.bfloat16)
    both = both.reshape(2, modes * vectors, local_k * LANES)
    depth = -(-modes * vectors // LANES) * LANES
    return jnp.pad(both, ((0, 0), (0, depth - modes * vectors), (0, 0)))


def shards(
    kpoint_coords,
    g_wannier,
    mode_vectors,
    frequencies,
    rotations,
    energies,
    band_window,
    target_owner,
    target_row,
):
    local_k = rotations.shape[0]
    bands = energies.shape[1]
    modes = frequencies.shape[1]
    vectors = g_wannier.shape[1]
    total_k = local_k * lax.axis_size("ka")
    g = lax.all_gather(g_wannier, "ka", axis=2, tiled=True)[0]
    mask_here = window_mask(band_window, bands)
    packed = jnp.concatenate([rotations, energies, mask_here.astype(jnp.bfloat16)], 1)
    gathered = lax.all_gather(packed, "ka", axis=0, tiled=True)
    wanted = target_owner[0, :, 0] * local_k + target_row[0]
    choose = (wanted[:, None] == jnp.arange(total_k, dtype=jnp.int32)[None, :]).astype(jnp.bfloat16)
    fetched = jnp.dot(choose, gathered, preferred_element_type=jnp.float32)
    size = 2 * bands * bands
    rot_there = fetched[:, :size].astype(jnp.bfloat16).reshape(local_k, 2, bands, bands)
    e_there = fetched[:, size : size + bands]
    mask_there = fetched[:, size + bands :]

    weights = weights_of(
        phases_of(kpoint_coords, vectors).reshape(2, local_k, vectors), mode_vectors[0]
    )
    rot_here = rotations.reshape(local_k, 2, bands, bands)
    right = jnp.transpose(rot_here, (0, 3, 1, 2)).reshape(local_k, bands, 2 * bands)
    left = jnp.stack([rot_there[:, 0], -rot_there[:, 1]], 1)
    left = jnp.transpose(left, (0, 3, 1, 2)).reshape(local_k, bands, 2 * bands)

    e_here = energies.astype(jnp.float32)
    occ_here = occupation(e_here)
    occ_there = jnp.broadcast_to(occupation(e_there)[:, :, None], (local_k, bands, LANES))
    keep = jnp.broadcast_to(mask_there[:, :, None], (local_k, bands, LANES))
    frequency = frequencies[0]
    bose = 1.0 / (jnp.exp(frequency / THERMAL_KELVIN) - 1.0)
    ones = jnp.ones_like(bose)
    shift = lanes_of(frequency, -frequency)[None, None, :] - e_there[:, :, None]
    gain = keep * (lanes_of(bose, bose + 1.0) + lanes_of(ones, -ones) * occ_there)
    self_lanes, width_lanes = pair_sums(
        g, weights, right, left, e_here, occ_here * mask_here, mask_here, shift, gain, occ_there, keep, modes, bands
    )
    scale = SMEARING_WIDTH / math.pi
    self_part = jnp.sum(self_lanes, 2) * mask_here * (scale / lax.axis_size("pb"))
    width_part = jnp.sum(width_lanes, 0)[:modes] * (2.0 * math.pi / total_k * scale)
    electron_width = lax.psum(self_part, "pb")
    phonon_width = lax.psum(width_part, "ka")
    return (electron_width, phonon_width[None, :])


def solution(mesh):
    in_specs = (
        P(None, ("grp", "ka")),
        P(("grp", "pb"), None, "ka"),
        P(("grp", "pb"), None, None, None),
        P(("grp", "pb"), None),
        P(("grp", "ka"), None),
        P(("grp", "ka"), None),
        P(None, ("grp", "ka")),
        P(("grp", "pb"), "ka", None),
        P(("grp", "pb"), "ka"),
    )
    out_specs = (P(("grp", "ka"), None), P(("grp", "pb"), None))
    return jax.shard_map(shards, mesh=mesh, in_specs=in_specs, out_specs=out_specs, check_vma=False)
```

```python
import functools
import math

import jax
import jax.numpy as jnp
from jax import lax
from jax.experimental import pallas as pl
from jax.experimental.pallas import tpu as pltpu
from jax.sharding import PartitionSpec as P

THERMAL_KELVIN = 0.1
SMEARING_WIDTH = 0.05
LANES = 128
HALF = 64


def window_mask(band_window, bands):
    energy_levels = jnp.arange(bands, dtype=jnp.int32)
    inside = (energy_levels[None, :] >= band_window[0][:, None]) & (
        energy_levels[None, :] < band_window[1][:, None]
    )
    return inside.astype(jnp.float32)


def phases_of(coords, vectors):
    index = jnp.arange(vectors, dtype=jnp.int32)
    first = (index % 2).astype(jnp.float32)
    second = (index // 2 % 2).astype(jnp.float32)
    third = (index // 4 % 2).astype(jnp.float32)
    angle = coords[0][:, None] * first[None, :] + coords[1][:, None] * second[None, :]
    angle = 2.0 * math.pi * (angle + coords[2][:, None] * third[None, :])
    return jnp.concatenate([jnp.cos(angle), jnp.sin(angle)], 0).astype(jnp.bfloat16)


def occupation(energy_value):
    return 1.0 / (1.0 + jnp.exp(energy_value / THERMAL_KELVIN))


def pair_kernel(
    g_ref, w_ref, right_ref, left_ref, e_ref, up_ref, mask_ref, shift_ref, gain_ref, occ_ref, keep_ref,
    self_ref, width_ref, turned, modal, half, *, modes, bands
):
    area = bands * bands
    vectors = g_ref.shape[0]
    blocks = 2 * area // LANES
    per = LANES // vectors
    step = pl.program_id(0)

    @pl.when(step == 0)
    def _():
        width_ref[...] = jnp.zeros_like(width_ref)

        def turn(j, carry):
            for group in range(turned.shape[1] // LANES):
                rows = []
                for p in range(group * per, group * per + per):
                    if p < modes:
                        at = pl.multiple_of(p * 2 * area + j * LANES, LANES)
                        rows.append(g_ref[:, pl.ds(at, LANES)].astype(jnp.float32))
                    else:
                        rows.append(jnp.zeros((vectors, LANES), jnp.float32))
                tile = jnp.concatenate(rows, 0).T
                spot = pl.ds(pl.multiple_of(j * LANES, LANES), LANES)
                turned[spot, group * LANES : (group + 1) * LANES] = tile.astype(jnp.bfloat16)
            return carry

        lax.fori_loop(0, blocks, turn, 0)

    chunk = 8 * bands

    for c in range(area // chunk):
        first = c * chunk
        both = jnp.dot(turned[first : first + chunk, :], w_ref[0], preferred_element_type=jnp.float32)
        both += jnp.dot(
            turned[area + first : area + first + chunk, :], w_ref[1], preferred_element_type=jnp.float32
        )
        for kk in range(2):
            modal[kk, first : first + chunk, :] = both[:, kk * LANES : (kk + 1) * LANES]

    lane = lax.broadcasted_iota(jnp.int32, (bands, LANES), 1)
    sign = jnp.where(lane < HALF, -1.0, 1.0)

    def operand(block):
        block = jnp.concatenate([block, pltpu.roll(block, HALF, 1) * sign], 0)
        return block.astype(jnp.bfloat16)

    def one_k(kk, carry):
        k = step * 2 + kk
        right = right_ref[kk]
        for a in range(0, bands, 2):
            pair = [operand(modal[kk, (a + s) * bands : (a + s + 1) * bands, :]) for s in range(2)]
            out = jnp.dot(right, jnp.concatenate(pair, 1), preferred_element_type=jnp.float32)
            for s in range(2):
                half[pl.ds(a + s, bands, stride=bands), :] = out[:, s * LANES : (s + 1) * LANES]
        left = left_ref[kk]
        shift = shift_ref[kk]
        gain = gain_ref[kk]
        occ = occ_ref[kk]
        total = jnp.zeros((bands, LANES), jnp.float32)
        for n in range(0, bands, 2):
            pair = [operand(half[(n + s) * bands : (n + s + 1) * bands, :]) for s in range(2)]
            out = jnp.dot(left, jnp.concatenate(pair, 1), preferred_element_type=jnp.float32)
            for s in range(2):
                coupling = out[:, s * LANES : (s + 1) * LANES]
                square = coupling * coupling
                strength = square + pltpu.roll(square, HALF, 1)
                x = shift + e_ref[k, n + s]
                term = strength / (x * x + SMEARING_WIDTH * SMEARING_WIDTH)
                self_ref[kk, n + s : n + s + 1, :] = jnp.sum(term * gain, 0, keepdims=True)
                total += term * (up_ref[k, n + s] - mask_ref[k, n + s] * occ)
        width_ref[...] += total * keep_ref[kk]
        return carry

    lax.fori_loop(0, 2, one_k, 0)


def pair_sums(g, weights, right, left, e_here, up_here, mask_here, shift, gain, occ, keep, modes, bands):
    local_k = right.shape[0]
    depth = weights.shape[1]
    area = bands * bands
    by_k = lambda i: (i, 0, 0)
    table = pl.BlockSpec((2, bands, LANES), by_k)
    return pl.pallas_call(
        functools.partial(pair_kernel, modes=modes, bands=bands),
        grid=(local_k // 2,),
        in_specs=[
            pl.BlockSpec(g.shape, lambda i: (0, 0)),
            pl.BlockSpec((2, depth, 2 * LANES), lambda i: (0, 0, i)),
            pl.BlockSpec((2,) + right.shape[1:], by_k),
            pl.BlockSpec((2,) + left.shape[1:], by_k),
            pl.BlockSpec(memory_space=pltpu.SMEM),
            pl.BlockSpec(memory_space=pltpu.SMEM),
            pl.BlockSpec(memory_space=pltpu.SMEM),
            table,
            table,
            table,
            table,
        ],
        out_specs=[table, pl.BlockSpec((bands, LANES), lambda i: (0, 0))],
        out_shape=[
            jax.ShapeDtypeStruct((local_k, bands, LANES), jnp.float32),
            jax.ShapeDtypeStruct((bands, LANES), jnp.float32),
        ],
        scratch_shapes=[
            pltpu.VMEM((2 * area, depth), jnp.bfloat16),
            pltpu.VMEM((2, area, LANES), jnp.float32),
            pltpu.VMEM((area, LANES), jnp.float32),
        ],
        compiler_params=pltpu.CompilerParams(vmem_limit_bytes=48 * 1024 * 1024),
        name="pairs",
    )(g, weights, right, left, e_here, up_here, mask_here, shift, gain, occ, keep)


def sum_kernel(sizes, self_ref, width_ref, self_out, width_out, self_slots, width_slots, sends, receives):
    kinds = (("pb", sizes[0], self_ref, self_slots), ("ka", sizes[1], width_ref, width_slots))
    barrier = pltpu.get_barrier_semaphore()
    for axis, size, _, _ in kinds:
        for hop in range(1, size):
            peer = lax.rem(lax.axis_index(axis) + hop, size)
            pl.semaphore_signal(barrier, inc=1, device_id={axis: peer}, device_id_type=pl.DeviceIdType.MESH)
    pl.semaphore_wait(barrier, sizes[0] + sizes[1] - 2)
    copies = []
    for axis, size, source, slots in kinds:
        me = lax.axis_index(axis)
        for hop in range(1, size):
            copy = pltpu.make_async_remote_copy(
                src_ref=source,
                dst_ref=slots.at[me],
                send_sem=sends.at[len(copies)],
                recv_sem=receives.at[len(copies)],
                device_id={axis: lax.rem(me + hop, size)},
                device_id_type=pl.DeviceIdType.MESH,
            )
            copy.start()
            copies.append(copy)
        slots[me] = source[...]
    for copy in copies:
        copy.wait()
    for (_, size, _, slots), out in zip(kinds, (self_out, width_out)):
        total = slots[0]
        for s in range(1, size):
            total += slots[s]
        out[...] = total


def both_sums(self_part, width_part):
    sizes = (lax.axis_size("pb"), lax.axis_size("ka"))
    copies = sizes[0] + sizes[1] - 2
    return pl.pallas_call(
        functools.partial(sum_kernel, sizes),
        in_specs=[pl.BlockSpec(memory_space=pltpu.VMEM)] * 2,
        out_specs=[pl.BlockSpec(memory_space=pltpu.VMEM)] * 2,
        out_shape=[jax.ShapeDtypeStruct(a.shape, jnp.float32) for a in (self_part, width_part)],
        scratch_shapes=[
            pltpu.VMEM((sizes[0],) + self_part.shape, jnp.float32),
            pltpu.VMEM((sizes[1],) + width_part.shape, jnp.float32),
            pltpu.SemaphoreType.DMA((copies,)),
            pltpu.SemaphoreType.DMA((copies,)),
        ],
        compiler_params=pltpu.CompilerParams(collective_id=0, has_side_effects=True),
        name="sums",
    )(self_part, width_part)


def lanes_of(first, second):
    pad = [(0, 0)] * (first.ndim - 1) + [(0, HALF - first.shape[-1])]
    return jnp.concatenate([jnp.pad(first, pad), jnp.pad(second, pad)], -1)


def weights_of(phases, mode_pair):
    _, local_k, vectors = phases.shape
    modes = mode_pair.shape[1]
    wave = phases.astype(jnp.float32)
    vec = mode_pair.astype(jnp.float32).reshape(2, modes // 2, 2, modes)
    vec = jnp.transpose(vec, (0, 2, 1, 3))[:, :, :, None, None, :]
    cos, sin = (jnp.transpose(w)[None, None, :, :, None] for w in (wave[0], wave[1]))
    real = cos * vec[0] - sin * vec[1]
    imag = cos * vec[1] + sin * vec[0]
    both = jnp.stack([lanes_of(real, imag), lanes_of(-imag, real)], 1).astype(jnp.bfloat16)
    both = both.reshape(2, modes * vectors, local_k * LANES)
    depth = -(-modes * vectors // LANES) * LANES
    return jnp.pad(both, ((0, 0), (0, depth - modes * vectors), (0, 0)))


def shards(
    kpoint_coords,
    g_wannier,
    mode_vectors,
    frequencies,
    rotations,
    energies,
    band_window,
    target_owner,
    target_row,
):
    local_k = rotations.shape[0]
    bands = energies.shape[1]
    modes = frequencies.shape[1]
    vectors = g_wannier.shape[1]
    total_k = local_k * lax.axis_size("ka")
    g = lax.all_gather(g_wannier, "ka", axis=2, tiled=True)[0]
    mask_here = window_mask(band_window, bands)
    packed = jnp.concatenate([rotations, energies, mask_here.astype(jnp.bfloat16)], 1)
    share = local_k // lax.axis_size("pb")
    mine = lax.dynamic_slice_in_dim(packed, lax.axis_index("pb") * share, share, 0)
    gathered = lax.all_gather(mine, ("ka", "pb"), axis=0, tiled=True)
    wanted = target_owner[0, :, 0] * local_k + target_row[0]
    choose = (wanted[:, None] == jnp.arange(total_k, dtype=jnp.int32)[None, :]).astype(jnp.bfloat16)
    fetched = jnp.dot(choose, gathered, preferred_element_type=jnp.float32)
    size = 2 * bands * bands
    rot_there = fetched[:, :size].astype(jnp.bfloat16).reshape(local_k, 2, bands, bands)
    e_there = fetched[:, size : size + bands]
    mask_there = fetched[:, size + bands :]

    weights = weights_of(
        phases_of(kpoint_coords, vectors).reshape(2, local_k, vectors), mode_vectors[0]
    )
    rot_here = rotations.reshape(local_k, 2, bands, bands)
    right = jnp.transpose(rot_here, (0, 3, 1, 2)).reshape(local_k, bands, 2 * bands)
    left = jnp.stack([rot_there[:, 0], -rot_there[:, 1]], 1)
    left = jnp.transpose(left, (0, 3, 1, 2)).reshape(local_k, bands, 2 * bands)

    e_here = energies.astype(jnp.float32)
    occ_here = occupation(e_here)
    occ_there = jnp.broadcast_to(occupation(e_there)[:, :, None], (local_k, bands, LANES))
    keep = jnp.broadcast_to(mask_there[:, :, None], (local_k, bands, LANES))
    frequency = frequencies[0]
    bose = 1.0 / (jnp.exp(frequency / THERMAL_KELVIN) - 1.0)
    ones = jnp.ones_like(bose)
    shift = lanes_of(frequency, -frequency)[None, None, :] - e_there[:, :, None]
    gain = keep * (lanes_of(bose, bose + 1.0) + lanes_of(ones, -ones) * occ_there)
    self_lanes, width_lanes = pair_sums(
        g, weights, right, left, e_here, occ_here * mask_here, mask_here, shift, gain, occ_there, keep, modes, bands
    )
    scale = SMEARING_WIDTH / math.pi
    self_part = jnp.sum(self_lanes, 2) * mask_here * (scale / lax.axis_size("pb"))
    width_part = jnp.sum(width_lanes, 0)[:modes] * (2.0 * math.pi / total_k * scale)
    self_part = jnp.pad(self_part, ((0, 0), (0, LANES - bands)))
    width_part = jnp.broadcast_to(jnp.pad(width_part, (0, LANES - modes))[None, :], (8, LANES))
    electron_width, phonon_width = both_sums(self_part, width_part)
    return (electron_width[:, :bands], phonon_width[:1, :modes])


def solution(mesh):
    in_specs = (
        P(None, ("grp", "ka")),
        P(("grp", "pb"), None, "ka"),
        P(("grp", "pb"), None, None, None),
        P(("grp", "pb"), None),
        P(("grp", "ka"), None),
        P(("grp", "ka"), None),
        P(None, ("grp", "ka")),
        P(("grp", "pb"), "ka", None),
        P(("grp", "pb"), "ka"),
    )
    out_specs = (P(("grp", "ka"), None), P(("grp", "pb"), None))
    return jax.shard_map(shards, mesh=mesh, in_specs=in_specs, out_specs=out_specs, check_vma=False)
```

```python
import functools
import math

import jax
import jax.numpy as jnp
from jax import lax
from jax.experimental import pallas as pl
from jax.experimental.pallas import tpu as pltpu
from jax.sharding import PartitionSpec as P

THERMAL_KELVIN = 0.1
SMEARING_WIDTH = 0.05
LANES = 128
HALF = 64


def window_mask(band_window, bands):
    energy_levels = jnp.arange(bands, dtype=jnp.int32)
    inside = (energy_levels[None, :] >= band_window[0][:, None]) & (
        energy_levels[None, :] < band_window[1][:, None]
    )
    return inside.astype(jnp.float32)


def phases_of(coords, vectors):
    index = jnp.arange(vectors, dtype=jnp.int32)
    first = (index % 2).astype(jnp.float32)
    second = (index // 2 % 2).astype(jnp.float32)
    third = (index // 4 % 2).astype(jnp.float32)
    angle = coords[0][:, None] * first[None, :] + coords[1][:, None] * second[None, :]
    angle = 2.0 * math.pi * (angle + coords[2][:, None] * third[None, :])
    return jnp.concatenate([jnp.cos(angle), jnp.sin(angle)], 0).astype(jnp.bfloat16)


def occupation(energy_value):
    return 1.0 / (1.0 + jnp.exp(energy_value / THERMAL_KELVIN))


def turn_part(g_ref, turned, area):
    vectors, length = g_ref.shape
    pairs = length // (2 * area)
    fill = jnp.zeros((LANES - pairs * vectors, LANES), jnp.float32)

    def turn(j, carry):
        rows = [
            g_ref[:, pl.ds(pl.multiple_of(p * 2 * area + j * LANES, LANES), LANES)].astype(jnp.float32)
            for p in range(pairs)
        ]
        tile = jnp.concatenate(rows + [fill], 0).T.astype(jnp.bfloat16)
        spot = pl.multiple_of(j * LANES, LANES)
        for half in range(LANES // HALF):
            first = spot + half * HALF

            @pl.when(first < area)
            def _():
                turned[pl.ds(pl.multiple_of(first, HALF), HALF), :LANES] = tile[half * HALF : (half + 1) * HALF]

            @pl.when(first >= area)
            def _():
                later = pl.multiple_of(first - area, HALF)
                turned[pl.ds(later, HALF), LANES:] = tile[half * HALF : (half + 1) * HALF]

        return carry

    lax.fori_loop(0, 2 * area // LANES, turn, 0)


def early_kernel(*refs, area):
    order_ref, parts, w_ref, out_ref, turned = refs[0], refs[1:-3], refs[-3], refs[-2], refs[-1]

    @pl.when(pl.program_id(0) == 0)
    def _():
        for s, g_ref in enumerate(parts):
            turn_part(g_ref, turned.at[s], area)

    chunk = area // 5
    for c in range(5):
        rows = slice(c * chunk, (c + 1) * chunk)
        total = 0.0
        for s in range(len(parts)):
            total += jnp.dot(turned[s, rows, :], w_ref[order_ref[s]], preferred_element_type=jnp.float32)
        out_ref[rows, :] = total


def early_sums(order, parts, weights, area):
    count, depth, width = weights.shape
    return pl.pallas_call(
        functools.partial(early_kernel, area=area),
        grid=(width // (2 * LANES),),
        in_specs=[pl.BlockSpec(memory_space=pltpu.SMEM)]
        + [pl.BlockSpec(g.shape, lambda i: (0, 0)) for g in parts]
        + [pl.BlockSpec((count, depth, 2 * LANES), lambda i: (0, 0, i))],
        out_specs=pl.BlockSpec((area, 2 * LANES), lambda i: (0, i)),
        out_shape=jax.ShapeDtypeStruct((area, width), jnp.float32),
        scratch_shapes=[pltpu.VMEM((len(parts), area, depth), jnp.bfloat16)],
        compiler_params=pltpu.CompilerParams(vmem_limit_bytes=48 * 1024 * 1024),
        cost_estimate=pl.CostEstimate(
            flops=2 * len(parts) * area * depth * width,
            bytes_accessed=4 * area * width + 2 * weights.size,
            transcendentals=0,
        ),
        name="early",
    )(order, *parts, weights)


def pair_kernel(
    order_ref, g_ref, w_ref, early_ref, right_ref, left_ref, e_ref, up_ref, mask_ref,
    shift_ref, gain_ref, occ_ref, keep_ref, self_ref, width_ref, turned, modal, half, *, bands
):
    area = bands * bands
    step = pl.program_id(0)

    @pl.when(step == 0)
    def _():
        width_ref[...] = jnp.zeros_like(width_ref)
        turn_part(g_ref, turned, area)

    chunk = 8 * bands
    weight = w_ref[order_ref[w_ref.shape[0] - 1]]

    for c in range(area // chunk):
        first = c * chunk
        both = early_ref[first : first + chunk, :] + jnp.dot(
            turned[first : first + chunk, :], weight, preferred_element_type=jnp.float32
        )
        for kk in range(2):
            modal[kk, first : first + chunk, :] = both[:, kk * LANES : (kk + 1) * LANES]

    lane = lax.broadcasted_iota(jnp.int32, (bands, LANES), 1)
    sign = jnp.where(lane < HALF, -1.0, 1.0)

    def operand(block):
        block = jnp.concatenate([block, pltpu.roll(block, HALF, 1) * sign], 0)
        return block.astype(jnp.bfloat16)

    def one_k(kk, carry):
        k = step * 2 + kk
        right = right_ref[kk]
        for a in range(0, bands, 2):
            pair = [operand(modal[kk, (a + s) * bands : (a + s + 1) * bands, :]) for s in range(2)]
            out = jnp.dot(right, jnp.concatenate(pair, 1), preferred_element_type=jnp.float32)
            for s in range(2):
                half[pl.ds(a + s, bands, stride=bands), :] = out[:, s * LANES : (s + 1) * LANES]
        left = left_ref[kk]
        shift = shift_ref[kk]
        gain = gain_ref[kk]
        occ = occ_ref[kk]
        total = jnp.zeros((bands, LANES), jnp.float32)
        for n in range(0, bands, 2):
            pair = [operand(half[(n + s) * bands : (n + s + 1) * bands, :]) for s in range(2)]
            out = jnp.dot(left, jnp.concatenate(pair, 1), preferred_element_type=jnp.float32)
            for s in range(2):
                coupling = out[:, s * LANES : (s + 1) * LANES]
                square = coupling * coupling
                strength = square + pltpu.roll(square, HALF, 1)
                x = shift + e_ref[k, n + s]
                term = strength / (x * x + SMEARING_WIDTH * SMEARING_WIDTH)
                self_ref[kk, n + s : n + s + 1, :] = jnp.sum(term * gain, 0, keepdims=True)
                total += term * (up_ref[k, n + s] - mask_ref[k, n + s] * occ)
        width_ref[...] += total * keep_ref[kk]
        return carry

    lax.fori_loop(0, 2, one_k, 0)


def pair_sums(order, g, weights, early, right, left, e_here, up_here, mask_here, shift, gain, occ, keep, bands):
    local_k = right.shape[0]
    count, depth, _ = weights.shape
    area = bands * bands
    by_k = lambda i: (i, 0, 0)
    table = pl.BlockSpec((2, bands, LANES), by_k)
    return pl.pallas_call(
        functools.partial(pair_kernel, bands=bands),
        grid=(local_k // 2,),
        in_specs=[
            pl.BlockSpec(memory_space=pltpu.SMEM),
            pl.BlockSpec(g.shape, lambda i: (0, 0)),
            pl.BlockSpec((count, depth, 2 * LANES), lambda i: (0, 0, i)),
            pl.BlockSpec((area, 2 * LANES), lambda i: (0, i)),
            pl.BlockSpec((2,) + right.shape[1:], by_k),
            pl.BlockSpec((2,) + left.shape[1:], by_k),
            pl.BlockSpec(memory_space=pltpu.SMEM),
            pl.BlockSpec(memory_space=pltpu.SMEM),
            pl.BlockSpec(memory_space=pltpu.SMEM),
            table,
            table,
            table,
            table,
        ],
        out_specs=[table, pl.BlockSpec((bands, LANES), lambda i: (0, 0))],
        out_shape=[
            jax.ShapeDtypeStruct((local_k, bands, LANES), jnp.float32),
            jax.ShapeDtypeStruct((bands, LANES), jnp.float32),
        ],
        scratch_shapes=[
            pltpu.VMEM((area, depth), jnp.bfloat16),
            pltpu.VMEM((2, area, LANES), jnp.float32),
            pltpu.VMEM((area, LANES), jnp.float32),
        ],
        compiler_params=pltpu.CompilerParams(vmem_limit_bytes=48 * 1024 * 1024),
        name="pairs",
    )(order, g, weights, early, right, left, e_here, up_here, mask_here, shift, gain, occ, keep)


def sum_kernel(sizes, self_ref, width_ref, self_out, width_out, self_slots, width_slots, sends, receives):
    kinds = (("pb", sizes[0], self_ref, self_slots), ("ka", sizes[1], width_ref, width_slots))
    barrier = pltpu.get_barrier_semaphore()
    for axis, size, _, _ in kinds:
        for hop in range(1, size):
            peer = lax.rem(lax.axis_index(axis) + hop, size)
            pl.semaphore_signal(barrier, inc=1, device_id={axis: peer}, device_id_type=pl.DeviceIdType.MESH)
    pl.semaphore_wait(barrier, sizes[0] + sizes[1] - 2)
    copies = []
    for axis, size, source, slots in kinds:
        me = lax.axis_index(axis)
        for hop in range(1, size):
            copy = pltpu.make_async_remote_copy(
                src_ref=source,
                dst_ref=slots.at[me],
                send_sem=sends.at[len(copies)],
                recv_sem=receives.at[len(copies)],
                device_id={axis: lax.rem(me + hop, size)},
                device_id_type=pl.DeviceIdType.MESH,
            )
            copy.start()
            copies.append(copy)
        slots[me] = source[...]
    for copy in copies:
        copy.wait()
    for (_, size, _, slots), out in zip(kinds, (self_out, width_out)):
        total = slots[0]
        for s in range(1, size):
            total += slots[s]
        out[...] = total


def both_sums(self_part, width_part):
    sizes = (lax.axis_size("pb"), lax.axis_size("ka"))
    copies = sizes[0] + sizes[1] - 2
    return pl.pallas_call(
        functools.partial(sum_kernel, sizes),
        in_specs=[pl.BlockSpec(memory_space=pltpu.VMEM)] * 2,
        out_specs=[pl.BlockSpec(memory_space=pltpu.VMEM)] * 2,
        out_shape=[jax.ShapeDtypeStruct(a.shape, jnp.float32) for a in (self_part, width_part)],
        scratch_shapes=[
            pltpu.VMEM((sizes[0],) + self_part.shape, jnp.float32),
            pltpu.VMEM((sizes[1],) + width_part.shape, jnp.float32),
            pltpu.SemaphoreType.DMA((copies,)),
            pltpu.SemaphoreType.DMA((copies,)),
        ],
        compiler_params=pltpu.CompilerParams(collective_id=0, has_side_effects=True),
        name="sums",
    )(self_part, width_part)


def lanes_of(first, second):
    pad = [(0, 0)] * (first.ndim - 1) + [(0, HALF - first.shape[-1])]
    return jnp.concatenate([jnp.pad(first, pad), jnp.pad(second, pad)], -1)


def weights_of(phases, mode_pair, pairs):
    _, local_k, vectors = phases.shape
    modes = mode_pair.shape[1]
    wave = phases.astype(jnp.float32)
    vec = mode_pair.astype(jnp.float32).reshape(2, modes // 2 // pairs, pairs, 2, modes)
    vec = jnp.transpose(vec, (0, 1, 3, 2, 4))[..., None, None, :]
    cos, sin = (jnp.transpose(w)[None, None, None, :, :, None] for w in (wave[0], wave[1]))
    real = cos * vec[0] - sin * vec[1]
    imag = cos * vec[1] + sin * vec[0]
    both = jnp.stack([lanes_of(real, imag), lanes_of(-imag, real)]).astype(jnp.bfloat16)
    both = both.reshape(modes // pairs, 2, pairs * vectors, local_k * LANES)
    both = jnp.pad(both, ((0, 0), (0, 0), (0, LANES - pairs * vectors), (0, 0)))
    return both.reshape(modes // pairs, 2 * LANES, local_k * LANES)


def ring_of(array, axis):
    size = lax.axis_size(axis)
    held = [array]
    for _ in range(size - 1):
        held.append(lax.ppermute(held[-1], axis, [(i, (i + 1) % size) for i in range(size)]))
    return held


def from_each(array, axis):
    size = lax.axis_size(axis)
    return [array] + [
        lax.ppermute(array, axis, [(i, (i + hop) % size) for i in range(size)]) for hop in range(1, size)
    ]


def shards(
    kpoint_coords,
    g_wannier,
    mode_vectors,
    frequencies,
    rotations,
    energies,
    band_window,
    target_owner,
    target_row,
):
    local_k = rotations.shape[0]
    bands = energies.shape[1]
    modes = frequencies.shape[1]
    vectors = g_wannier.shape[1]
    ka_size, pb_size = lax.axis_size("ka"), lax.axis_size("pb")
    ka, pb = lax.axis_index("ka"), lax.axis_index("pb")
    total_k = local_k * ka_size
    area = bands * bands
    pairs = max(n for n in range(1, LANES // vectors + 1) if modes // 2 % n == 0)
    count = modes // pairs
    mask_here = window_mask(band_window, bands)
    packed = jnp.concatenate([rotations, energies, mask_here.astype(jnp.bfloat16)], 1)
    share = local_k // pb_size
    mine = lax.dynamic_slice_in_dim(packed, pb * share, share, 0)
    mine = jnp.concatenate(from_each(mine, "ka"), 0)
    gathered = jnp.concatenate(from_each(mine, "pb"), 0)
    if ka_size == count:
        parts = ring_of(g_wannier[0], "ka")
        order = (ka - jnp.arange(count, dtype=jnp.int32)) % count
    else:
        whole = lax.all_gather(g_wannier, "ka", axis=2, tiled=True)[0]
        parts = jnp.split(whole, count, 1)
        order = jnp.arange(count, dtype=jnp.int32)
    owner, row = target_owner[0, :, 0], target_row[0]
    wanted = ((pb - row // share) % pb_size * ka_size + (ka - owner) % ka_size) * share + row % share
    choose = (wanted[:, None] == jnp.arange(total_k, dtype=jnp.int32)[None, :]).astype(jnp.bfloat16)
    fetched = jnp.dot(choose, gathered, preferred_element_type=jnp.float32)
    size = 2 * area
    rot_there = fetched[:, :size].astype(jnp.bfloat16).reshape(local_k, 2, bands, bands)
    e_there = fetched[:, size : size + bands]
    mask_there = fetched[:, size + bands :]

    weights = weights_of(
        phases_of(kpoint_coords, vectors).reshape(2, local_k, vectors), mode_vectors[0], pairs
    )
    early = early_sums(order, parts[:-1], weights, area)
    rot_here = rotations.reshape(local_k, 2, bands, bands)
    right = jnp.transpose(rot_here, (0, 3, 1, 2)).reshape(local_k, bands, 2 * bands)
    left = jnp.stack([rot_there[:, 0], -rot_there[:, 1]], 1)
    left = jnp.transpose(left, (0, 3, 1, 2)).reshape(local_k, bands, 2 * bands)

    e_here = energies.astype(jnp.float32)
    occ_here = occupation(e_here)
    occ_there = jnp.broadcast_to(occupation(e_there)[:, :, None], (local_k, bands, LANES))
    keep = jnp.broadcast_to(mask_there[:, :, None], (local_k, bands, LANES))
    frequency = frequencies[0]
    bose = 1.0 / (jnp.exp(frequency / THERMAL_KELVIN) - 1.0)
    ones = jnp.ones_like(bose)
    shift = lanes_of(frequency, -frequency)[None, None, :] - e_there[:, :, None]
    gain = keep * (lanes_of(bose, bose + 1.0) + lanes_of(ones, -ones) * occ_there)
    self_lanes, width_lanes = pair_sums(
        order, parts[-1], weights, early, right, left, e_here, occ_here * mask_here, mask_here,
        shift, gain, occ_there, keep, bands,
    )
    scale = SMEARING_WIDTH / math.pi
    self_part = jnp.sum(self_lanes, 2) * mask_here * (scale / pb_size)
    width_part = jnp.sum(width_lanes, 0)[:modes] * (2.0 * math.pi / total_k * scale)
    self_part = jnp.pad(self_part, ((0, 0), (0, LANES - bands)))
    width_part = jnp.broadcast_to(jnp.pad(width_part, (0, LANES - modes))[None, :], (8, LANES))
    electron_width, phonon_width = both_sums(self_part, width_part)
    return (electron_width[:, :bands], phonon_width[:1, :modes])


def solution(mesh):
    in_specs = (
        P(None, ("grp", "ka")),
        P(("grp", "pb"), None, "ka"),
        P(("grp", "pb"), None, None, None),
        P(("grp", "pb"), None),
        P(("grp", "ka"), None),
        P(("grp", "ka"), None),
        P(None, ("grp", "ka")),
        P(("grp", "pb"), "ka", None),
        P(("grp", "pb"), "ka"),
    )
    out_specs = (P(("grp", "ka"), None), P(("grp", "pb"), None))
    return jax.shard_map(shards, mesh=mesh, in_specs=in_specs, out_specs=out_specs, check_vma=False)
```

```python
import functools
import math

import jax
import jax.numpy as jnp
from jax import lax
from jax.experimental import pallas as pl
from jax.experimental.pallas import tpu as pltpu
from jax.sharding import PartitionSpec as P

THERMAL_KELVIN = 0.1
SMEARING_WIDTH = 0.05
LANES = 128
HALF = 64
VMEM_LIMIT = 32 * 1024 * 1024


def window_mask(band_window, bands):
    energy_levels = jnp.arange(bands, dtype=jnp.int32)
    inside = (energy_levels[None, :] >= band_window[0][:, None]) & (
        energy_levels[None, :] < band_window[1][:, None]
    )
    return inside.astype(jnp.float32)


def phases_of(coords, vectors):
    index = jnp.arange(vectors, dtype=jnp.int32)
    first = (index % 2).astype(jnp.float32)
    second = (index // 2 % 2).astype(jnp.float32)
    third = (index // 4 % 2).astype(jnp.float32)
    angle = coords[0][:, None] * first[None, :] + coords[1][:, None] * second[None, :]
    angle = 2.0 * math.pi * (angle + coords[2][:, None] * third[None, :])
    return jnp.concatenate([jnp.cos(angle), jnp.sin(angle)], 0).astype(jnp.bfloat16)


def occupation(energy_value):
    return 1.0 / (1.0 + jnp.exp(energy_value / THERMAL_KELVIN))


def turn_part(g_ref, turned, area):
    vectors, length = g_ref.shape
    pairs = length // (2 * area)
    fill = jnp.zeros((LANES - pairs * vectors, LANES), jnp.float32)

    def tile_of(start):
        rows = [
            g_ref[:, pl.ds(pl.multiple_of(p * 2 * area + start, LANES), LANES)].astype(jnp.float32)
            for p in range(pairs)
        ]
        return jnp.concatenate(rows + [fill], 0).T.astype(jnp.bfloat16)

    whole = area // LANES
    rest = area - whole * LANES

    def even(j, carry):
        spot = pl.multiple_of(j * LANES, LANES)
        turned[pl.ds(spot, LANES), :LANES] = tile_of(spot)
        return carry

    def odd(j, carry):
        spot = pl.multiple_of(j * LANES, LANES)
        turned[pl.ds(pl.multiple_of(spot + LANES - rest, rest), LANES), LANES:] = tile_of(spot + (whole + 1) * LANES)
        return carry

    lax.fori_loop(0, whole, even, 0)
    middle = tile_of(whole * LANES)
    turned[whole * LANES : area, :LANES] = middle[:rest]
    turned[: LANES - rest, LANES:] = middle[rest:]
    lax.fori_loop(0, whole, odd, 0)


def early_kernel(*refs, area):
    order_ref, parts, w_ref, out_ref, turned = refs[0], refs[1:-3], refs[-3], refs[-2], refs[-1]
    for s, g_ref in enumerate(parts):
        turn_part(g_ref, turned.at[s], area)
    chunk = area // 5

    def one_step(step, carry):
        columns = pl.ds(pl.multiple_of(step * 2 * LANES, 2 * LANES), 2 * LANES)
        weights = [w_ref[order_ref[s], :, columns] for s in range(len(parts))]
        for c in range(5):
            rows = slice(c * chunk, (c + 1) * chunk)
            total = 0.0
            for s in range(len(parts)):
                total += jnp.dot(turned[s, rows, :], weights[s], preferred_element_type=jnp.float32)
            out_ref[step, rows, :] = total.astype(out_ref.dtype)
        return carry

    lax.fori_loop(0, out_ref.shape[0], one_step, 0)


def early_sums(order, parts, weights, area):
    count, depth, width = weights.shape
    return pl.pallas_call(
        functools.partial(early_kernel, area=area),
        in_specs=[pl.BlockSpec(memory_space=pltpu.SMEM)]
        + [pl.BlockSpec(memory_space=pltpu.VMEM)] * (len(parts) + 1),
        out_specs=pl.BlockSpec(memory_space=pltpu.VMEM),
        out_shape=jax.ShapeDtypeStruct((width // (2 * LANES), area, 2 * LANES), jnp.bfloat16),
        scratch_shapes=[pltpu.VMEM((len(parts), area, depth), jnp.bfloat16)],
        compiler_params=pltpu.CompilerParams(vmem_limit_bytes=VMEM_LIMIT),
        cost_estimate=pl.CostEstimate(
            flops=2 * len(parts) * area * depth * width,
            bytes_accessed=2 * area * width + 2 * weights.size,
            transcendentals=0,
        ),
        name="early",
    )(order, *parts, weights)


def pair_kernel(
    order_ref, g_ref, w_ref, early_ref, right_ref, left_ref, e_ref, up_ref, mask_ref,
    shift_ref, gain_ref, occ_ref, keep_ref, self_ref, width_ref, turned, modal, half, *, bands
):
    area = bands * bands
    width_ref[...] = jnp.zeros_like(width_ref)
    turn_part(g_ref, turned, area)
    chunk = 8 * bands
    lane = lax.broadcasted_iota(jnp.int32, (bands, LANES), 1)
    sign = jnp.where(lane < HALF, -1.0, 1.0)

    def operand(block):
        block = jnp.concatenate([block, pltpu.roll(block, HALF, 1) * sign], 0)
        return block.astype(jnp.bfloat16)

    def one_k(kk, step):
        k = step * 2 + kk
        right = right_ref[k]
        for a in range(0, bands, 2):
            pair = [operand(modal[kk, (a + s) * bands : (a + s + 1) * bands, :]) for s in range(2)]
            out = jnp.dot(right, jnp.concatenate(pair, 1), preferred_element_type=jnp.float32)
            for s in range(2):
                half[pl.ds(a + s, bands, stride=bands), :] = out[:, s * LANES : (s + 1) * LANES]
        left = left_ref[k]
        shift = shift_ref[k]
        gain = gain_ref[k]
        occ = occ_ref[k]
        total = jnp.zeros((bands, LANES), jnp.float32)
        for n in range(0, bands, 2):
            pair = [operand(half[(n + s) * bands : (n + s + 1) * bands, :]) for s in range(2)]
            out = jnp.dot(left, jnp.concatenate(pair, 1), preferred_element_type=jnp.float32)
            for s in range(2):
                coupling = out[:, s * LANES : (s + 1) * LANES]
                square = coupling * coupling
                strength = square + pltpu.roll(square, HALF, 1)
                x = shift + e_ref[k, n + s]
                term = strength / (x * x + SMEARING_WIDTH * SMEARING_WIDTH)
                self_ref[k, n + s : n + s + 1, :] = jnp.sum(term * gain, 0, keepdims=True)
                total += term * (up_ref[k, n + s] - mask_ref[k, n + s] * occ)
        width_ref[...] += total * keep_ref[k]
        return step

    def one_step(step, carry):
        columns = pl.ds(pl.multiple_of(step * 2 * LANES, 2 * LANES), 2 * LANES)
        weight = w_ref[order_ref[w_ref.shape[0] - 1], :, columns]
        for c in range(area // chunk):
            rows = slice(c * chunk, (c + 1) * chunk)
            both = early_ref[step, rows, :].astype(jnp.float32) + jnp.dot(
                turned[rows, :], weight, preferred_element_type=jnp.float32
            )
            for kk in range(2):
                modal[kk, rows, :] = both[:, kk * LANES : (kk + 1) * LANES]
        lax.fori_loop(0, 2, one_k, step)
        return carry

    lax.fori_loop(0, right_ref.shape[0] // 2, one_step, 0)


def pair_sums(order, g, weights, early, right, left, e_here, up_here, mask_here, shift, gain, occ, keep, bands):
    local_k = right.shape[0]
    depth = weights.shape[1]
    area = bands * bands
    vmem = pl.BlockSpec(memory_space=pltpu.VMEM)
    smem = pl.BlockSpec(memory_space=pltpu.SMEM)
    return pl.pallas_call(
        functools.partial(pair_kernel, bands=bands),
        in_specs=[smem] + [vmem] * 5 + [smem] * 3 + [vmem] * 4,
        out_specs=[vmem, vmem],
        out_shape=[
            jax.ShapeDtypeStruct((local_k, bands, LANES), jnp.float32),
            jax.ShapeDtypeStruct((bands, LANES), jnp.float32),
        ],
        scratch_shapes=[
            pltpu.VMEM((area, depth), jnp.bfloat16),
            pltpu.VMEM((2, area, LANES), jnp.float32),
            pltpu.VMEM((area, LANES), jnp.float32),
        ],
        compiler_params=pltpu.CompilerParams(vmem_limit_bytes=VMEM_LIMIT),
        name="pairs",
    )(order, g, weights, early, right, left, e_here, up_here, mask_here, shift, gain, occ, keep)


def greet(axes):
    barrier = pltpu.get_barrier_semaphore()
    for axis, size in axes:
        for hop in range(1, size):
            peer = lax.rem(lax.axis_index(axis) + hop, size)
            pl.semaphore_signal(barrier, inc=1, device_id={axis: peer}, device_id_type=pl.DeviceIdType.MESH)
    pl.semaphore_wait(barrier, sum(size - 1 for _, size in axes))


def send_all(axis, size, source, slots, sends, receives, first):
    me = lax.axis_index(axis)
    copies = []
    for hop in range(1, size):
        copy = pltpu.make_async_remote_copy(
            src_ref=source,
            dst_ref=slots.at[me],
            send_sem=sends.at[first + hop - 1],
            recv_sem=receives.at[first + hop - 1],
            device_id={axis: lax.rem(me + hop, size)},
            device_id_type=pl.DeviceIdType.MESH,
        )
        copy.start()
        copies.append(copy)
    slots[me] = source[...]
    return copies


def sum_kernel(
    sizes, scales, self_ref, mask_ref, width_ref, self_out, width_out,
    self_mine, width_mine, self_slots, width_slots, sends, receives
):
    self_mine[...] = jnp.sum(self_ref[...], 2) * mask_ref[...] * scales[0]
    width = jnp.sum(width_ref[...], 0, keepdims=True) * scales[1]
    width_mine[...] = jnp.broadcast_to(width, width_mine.shape)
    greet((("pb", sizes[0]), ("ka", sizes[1])))
    copies = send_all("pb", sizes[0], self_mine, self_slots, sends, receives, 0)
    copies += send_all("ka", sizes[1], width_mine, width_slots, sends, receives, sizes[0] - 1)
    for copy in copies:
        copy.wait()
    for size, slots, out in ((sizes[0], self_slots, self_out), (sizes[1], width_slots, width_out)):
        total = slots[0]
        for s in range(1, size):
            total += slots[s]
        out[...] = total[: out.shape[0], : out.shape[1]]


def both_sums(self_lanes, mask_here, width_lanes, modes, scales):
    sizes = (lax.axis_size("pb"), lax.axis_size("ka"))
    copies = sizes[0] + sizes[1] - 2
    return pl.pallas_call(
        functools.partial(sum_kernel, sizes, scales),
        in_specs=[pl.BlockSpec(memory_space=pltpu.VMEM)] * 3,
        out_specs=[pl.BlockSpec(memory_space=pltpu.VMEM)] * 2,
        out_shape=[
            jax.ShapeDtypeStruct(mask_here.shape, jnp.float32),
            jax.ShapeDtypeStruct((1, modes), jnp.float32),
        ],
        scratch_shapes=[
            pltpu.VMEM(mask_here.shape, jnp.float32),
            pltpu.VMEM((8, LANES), jnp.float32),
            pltpu.VMEM((sizes[0],) + mask_here.shape, jnp.float32),
            pltpu.VMEM((sizes[1], 8, LANES), jnp.float32),
            pltpu.SemaphoreType.DMA((copies,)),
            pltpu.SemaphoreType.DMA((copies,)),
        ],
        compiler_params=pltpu.CompilerParams(collective_id=0, has_side_effects=True),
        name="sums",
    )(self_lanes, mask_here, width_lanes)


def rows_kernel(sizes, mine_ref, out_ref, ka_slots, pb_slots, sends, receives):
    greet((("ka", sizes[1]), ("pb", sizes[0])))
    for copy in send_all("ka", sizes[1], mine_ref, ka_slots, sends, receives, 0):
        copy.wait()
    for copy in send_all("pb", sizes[0], ka_slots, pb_slots, sends, receives, sizes[1] - 1):
        copy.wait()
    rows, columns = mine_ref.shape
    for source in range(sizes[0]):
        for owner in range(sizes[1]):
            place = slice(owner * rows, (owner + 1) * rows), slice(source * columns, (source + 1) * columns)
            out_ref[place] = pb_slots[source, owner]


def gather_rows(packed):
    sizes = (lax.axis_size("pb"), lax.axis_size("ka"))
    rows, width = packed.shape
    columns = -(-width // (sizes[0] * LANES)) * LANES
    packed = jnp.pad(packed, ((0, 0), (0, columns * sizes[0] - width)))
    mine = lax.dynamic_slice_in_dim(packed, lax.axis_index("pb") * columns, columns, 1)
    copies = sizes[0] + sizes[1] - 2
    return pl.pallas_call(
        functools.partial(rows_kernel, sizes),
        in_specs=[pl.BlockSpec(memory_space=pltpu.VMEM)],
        out_specs=pl.BlockSpec(memory_space=pltpu.VMEM),
        out_shape=jax.ShapeDtypeStruct((sizes[1] * rows, sizes[0] * columns), packed.dtype),
        scratch_shapes=[
            pltpu.VMEM((sizes[1], rows, columns), packed.dtype),
            pltpu.VMEM((sizes[0], sizes[1], rows, columns), packed.dtype),
            pltpu.SemaphoreType.DMA((copies,)),
            pltpu.SemaphoreType.DMA((copies,)),
        ],
        compiler_params=pltpu.CompilerParams(collective_id=1, has_side_effects=True),
        name="rows",
    )(mine)


def lanes_of(first, second):
    pad = [(0, 0)] * (first.ndim - 1) + [(0, HALF - first.shape[-1])]
    return jnp.concatenate([jnp.pad(first, pad), jnp.pad(second, pad)], -1)


def weights_of(phases, mode_pair, pairs):
    _, local_k, vectors = phases.shape
    modes = mode_pair.shape[1]
    wave = phases.astype(jnp.float32)
    vec = mode_pair.astype(jnp.float32).reshape(2, modes // 2 // pairs, pairs, 2, modes)
    vec = jnp.transpose(vec, (0, 1, 3, 2, 4))[..., None, None, :]
    cos, sin = (jnp.transpose(w)[None, None, None, :, :, None] for w in (wave[0], wave[1]))
    real = cos * vec[0] - sin * vec[1]
    imag = cos * vec[1] + sin * vec[0]
    both = jnp.stack([lanes_of(real, imag), lanes_of(-imag, real)]).astype(jnp.bfloat16)
    both = both.reshape(modes // pairs, 2, pairs * vectors, local_k * LANES)
    both = jnp.pad(both, ((0, 0), (0, 0), (0, LANES - pairs * vectors), (0, 0)))
    return both.reshape(modes // pairs, 2 * LANES, local_k * LANES)


def ring_of(array, axis):
    size = lax.axis_size(axis)
    held = [array]
    for _ in range(size - 1):
        held.append(lax.ppermute(held[-1], axis, [(i, (i + 1) % size) for i in range(size)]))
    return held


def shards(
    kpoint_coords,
    g_wannier,
    mode_vectors,
    frequencies,
    rotations,
    energies,
    band_window,
    target_owner,
    target_row,
):
    local_k = rotations.shape[0]
    bands = energies.shape[1]
    modes = frequencies.shape[1]
    vectors = g_wannier.shape[1]
    ka_size, pb_size = lax.axis_size("ka"), lax.axis_size("pb")
    ka = lax.axis_index("ka")
    total_k = local_k * ka_size
    area = bands * bands
    pairs = max(n for n in range(1, LANES // vectors + 1) if modes // 2 % n == 0)
    count = modes // pairs
    mask_here = window_mask(band_window, bands)
    packed = jnp.concatenate([rotations, energies, mask_here.astype(jnp.bfloat16)], 1)
    gathered = gather_rows(packed)
    if ka_size == count:
        parts = ring_of(g_wannier[0], "ka")
        order = (ka - jnp.arange(count, dtype=jnp.int32)) % count
    else:
        whole = lax.all_gather(g_wannier, "ka", axis=2, tiled=True)[0]
        parts = jnp.split(whole, count, 1)
        order = jnp.arange(count, dtype=jnp.int32)
    wanted = target_owner[0, :, 0] * local_k + target_row[0]
    choose = (wanted[:, None] == jnp.arange(total_k, dtype=jnp.int32)[None, :]).astype(jnp.bfloat16)
    fetched = jnp.dot(choose, gathered, preferred_element_type=jnp.float32)
    size = 2 * area
    rot_there = fetched[:, :size].astype(jnp.bfloat16).reshape(local_k, 2, bands, bands)
    e_there = fetched[:, size : size + bands]
    mask_there = fetched[:, size + bands : size + 2 * bands]

    weights = weights_of(
        phases_of(kpoint_coords, vectors).reshape(2, local_k, vectors), mode_vectors[0], pairs
    )
    early = early_sums(order, parts[:-1], weights, area)
    rot_here = rotations.reshape(local_k, 2, bands, bands)
    right = jnp.transpose(rot_here, (0, 3, 1, 2)).reshape(local_k, bands, 2 * bands)
    left = jnp.stack([rot_there[:, 0], -rot_there[:, 1]], 1)
    left = jnp.transpose(left, (0, 3, 1, 2)).reshape(local_k, bands, 2 * bands)

    e_here = energies.astype(jnp.float32)
    occ_here = occupation(e_here)
    occ_there = jnp.broadcast_to(occupation(e_there)[:, :, None], (local_k, bands, LANES))
    keep = jnp.broadcast_to(mask_there[:, :, None], (local_k, bands, LANES))
    frequency = frequencies[0]
    bose = 1.0 / (jnp.exp(frequency / THERMAL_KELVIN) - 1.0)
    ones = jnp.ones_like(bose)
    shift = lanes_of(frequency, -frequency)[None, None, :] - e_there[:, :, None]
    gain = keep * (lanes_of(bose, bose + 1.0) + lanes_of(ones, -ones) * occ_there)
    self_lanes, width_lanes = pair_sums(
        order, parts[-1], weights, early, right, left, e_here, occ_here * mask_here, mask_here,
        shift, gain, occ_there, keep, bands,
    )
    scale = SMEARING_WIDTH / math.pi
    scales = (scale / pb_size, 2.0 * math.pi / total_k * scale)
    return both_sums(self_lanes, mask_here, width_lanes, modes, scales)


def solution(mesh):
    in_specs = (
        P(None, ("grp", "ka")),
        P(("grp", "pb"), None, "ka"),
        P(("grp", "pb"), None, None, None),
        P(("grp", "pb"), None),
        P(("grp", "ka"), None),
        P(("grp", "ka"), None),
        P(None, ("grp", "ka")),
        P(("grp", "pb"), "ka", None),
        P(("grp", "pb"), "ka"),
    )
    out_specs = (P(("grp", "ka"), None), P(("grp", "pb"), None))
    return jax.shard_map(shards, mesh=mesh, in_specs=in_specs, out_specs=out_specs, check_vma=False)
```

```python
import functools
import math

import jax
import jax.numpy as jnp
from jax import lax
from jax.experimental import pallas as pl
from jax.experimental.pallas import tpu as pltpu
from jax.sharding import PartitionSpec as P

THERMAL_KELVIN = 0.1
SMEARING_WIDTH = 0.05
LANES = 128
HALF = 64
VMEM_LIMIT = 32 * 1024 * 1024


def window_mask(band_window, bands):
    energy_levels = jnp.arange(bands, dtype=jnp.int32)
    inside = (energy_levels[None, :] >= band_window[0][:, None]) & (
        energy_levels[None, :] < band_window[1][:, None]
    )
    return inside.astype(jnp.float32)


def phases_of(coords, vectors):
    index = jnp.arange(vectors, dtype=jnp.int32)
    first = (index % 2).astype(jnp.float32)
    second = (index // 2 % 2).astype(jnp.float32)
    third = (index // 4 % 2).astype(jnp.float32)
    angle = coords[0][:, None] * first[None, :] + coords[1][:, None] * second[None, :]
    angle = 2.0 * math.pi * (angle + coords[2][:, None] * third[None, :])
    return jnp.concatenate([jnp.cos(angle), jnp.sin(angle)], 0).astype(jnp.bfloat16)


def occupation(energy_value):
    return 1.0 / (1.0 + jnp.exp(energy_value / THERMAL_KELVIN))


def turn_part(g_ref, turned, area):
    vectors, length = g_ref.shape
    pairs = length // (2 * area)
    fill = jnp.zeros((LANES - pairs * vectors, LANES), jnp.float32)

    def tile_of(start):
        rows = [
            g_ref[:, pl.ds(pl.multiple_of(p * 2 * area + start, LANES), LANES)].astype(jnp.float32)
            for p in range(pairs)
        ]
        return jnp.concatenate(rows + [fill], 0).T.astype(jnp.bfloat16)

    whole = area // LANES
    rest = area - whole * LANES

    def even(j, carry):
        spot = pl.multiple_of(j * LANES, LANES)
        turned[pl.ds(spot, LANES), :LANES] = tile_of(spot)
        return carry

    def odd(j, carry):
        spot = pl.multiple_of(j * LANES, LANES)
        turned[pl.ds(pl.multiple_of(spot + LANES - rest, rest), LANES), LANES:] = tile_of(spot + (whole + 1) * LANES)
        return carry

    lax.fori_loop(0, whole, even, 0)
    middle = tile_of(whole * LANES)
    turned[whole * LANES : area, :LANES] = middle[:rest]
    turned[: LANES - rest, LANES:] = middle[rest:]
    lax.fori_loop(0, whole, odd, 0)


def early_kernel(*refs, area):
    order_ref, parts, w_ref, out_ref, turned = refs[0], refs[1:-3], refs[-3], refs[-2], refs[-1]
    for s, g_ref in enumerate(parts):
        turn_part(g_ref, turned.at[s], area)
    chunk = area // 5

    def one_step(step, carry):
        columns = pl.ds(pl.multiple_of(step * 2 * LANES, 2 * LANES), 2 * LANES)
        weights = [w_ref[order_ref[s], :, columns] for s in range(len(parts))]
        for c in range(5):
            rows = slice(c * chunk, (c + 1) * chunk)
            total = 0.0
            for s in range(len(parts)):
                total += jnp.dot(turned[s, rows, :], weights[s], preferred_element_type=jnp.float32)
            out_ref[step, rows, :] = total.astype(out_ref.dtype)
        return carry

    lax.fori_loop(0, out_ref.shape[0], one_step, 0)


def early_sums(order, parts, weights, area):
    count, depth, width = weights.shape
    return pl.pallas_call(
        functools.partial(early_kernel, area=area),
        in_specs=[pl.BlockSpec(memory_space=pltpu.SMEM)]
        + [pl.BlockSpec(memory_space=pltpu.VMEM)] * (len(parts) + 1),
        out_specs=pl.BlockSpec(memory_space=pltpu.VMEM),
        out_shape=jax.ShapeDtypeStruct((width // (2 * LANES), area, 2 * LANES), jnp.bfloat16),
        scratch_shapes=[pltpu.VMEM((len(parts), area, depth), jnp.bfloat16)],
        compiler_params=pltpu.CompilerParams(vmem_limit_bytes=VMEM_LIMIT),
        cost_estimate=pl.CostEstimate(
            flops=2 * len(parts) * area * depth * width,
            bytes_accessed=2 * area * width + 2 * weights.size,
            transcendentals=0,
        ),
        name="early",
    )(order, *parts, weights)


def pair_kernel(
    order_ref, g_ref, w_ref, early_ref, right_ref, left_ref, e_ref, up_ref, mask_ref,
    shift_ref, gain_ref, occ_ref, keep_ref, self_ref, width_ref, turned, modal_even, modal_odd, half_even, half_odd, *, bands
):
    area = bands * bands
    steps = right_ref.shape[0] // 2
    modals, halves = (modal_even, modal_odd), (half_even, half_odd)
    width_ref[...] = jnp.zeros_like(width_ref)
    turn_part(g_ref, turned, area)
    lane = lax.broadcasted_iota(jnp.int32, (bands, LANES), 1)
    sign = jnp.where(lane < HALF, -1.0, 1.0)

    def operand(block):
        block = jnp.concatenate([block, pltpu.roll(block, HALF, 1) * sign], 0)
        return block.astype(jnp.bfloat16)

    def modal_of(t, modal, c):
        columns = pl.ds(pl.multiple_of(t * 2 * LANES, 2 * LANES), 2 * LANES)
        weight = w_ref[order_ref[w_ref.shape[0] - 1], :, columns]
        rows = slice(c * 8 * bands, (c + 1) * 8 * bands)
        both = early_ref[t, rows, :].astype(jnp.float32) + jnp.dot(
            turned[rows, :], weight, preferred_element_type=jnp.float32
        )
        for kk in range(2):
            modal[kk, rows, :] = both[:, kk * LANES : (kk + 1) * LANES]

    def half_of(k, kk, a, modal, half):
        pair = [operand(modal[kk, (a + s) * bands : (a + s + 1) * bands, :]) for s in range(2)]
        out = jnp.dot(right_ref[k], jnp.concatenate(pair, 1), preferred_element_type=jnp.float32)
        for s in range(2):
            half[kk, pl.ds(a + s, bands, stride=bands), :] = out[:, s * LANES : (s + 1) * LANES]

    def coupling_of(k, kk, n, half, total):
        pair = [operand(half[kk, (n + s) * bands : (n + s + 1) * bands, :]) for s in range(2)]
        out = jnp.dot(left_ref[k], jnp.concatenate(pair, 1), preferred_element_type=jnp.float32)
        for s in range(2):
            coupling = out[:, s * LANES : (s + 1) * LANES]
            square = coupling * coupling
            strength = square + pltpu.roll(square, HALF, 1)
            x = shift_ref[k] + e_ref[k, n + s]
            term = strength / (x * x + SMEARING_WIDTH * SMEARING_WIDTH)
            self_ref[k, n + s : n + s + 1, :] = jnp.sum(term * gain_ref[k], 0, keepdims=True)
            total += term * (up_ref[k, n + s] - mask_ref[k, n + s] * occ_ref[k])
        return total

    def run(t, slot, first, second, third):
        totals = [jnp.zeros((bands, LANES), jnp.float32)] * 2
        for i in range(0, bands, 2):
            if first and i % 8 == 0:
                modal_of(t, modals[slot], i // 8)
            for kk in range(2):
                if second:
                    half_of((t - 1) * 2 + kk, kk, i, modals[1 - slot], halves[1 - slot])
                if third:
                    totals[kk] = coupling_of((t - 2) * 2 + kk, kk, i, halves[slot], totals[kk])
        if third:
            for kk in range(2):
                width_ref[...] += totals[kk] * keep_ref[(t - 2) * 2 + kk]

    def two_steps(u, carry):
        run(2 * u, 0, True, True, True)
        run(2 * u + 1, 1, True, True, True)
        return carry

    run(0, 0, True, False, False)
    run(1, 1, True, True, False)
    lax.fori_loop(1, steps // 2, two_steps, 0)
    run(steps, 0, False, True, True)
    run(steps + 1, 1, False, False, True)


def pair_sums(order, g, weights, early, right, left, e_here, up_here, mask_here, shift, gain, occ, keep, bands):
    local_k = right.shape[0]
    depth = weights.shape[1]
    area = bands * bands
    vmem = pl.BlockSpec(memory_space=pltpu.VMEM)
    smem = pl.BlockSpec(memory_space=pltpu.SMEM)
    return pl.pallas_call(
        functools.partial(pair_kernel, bands=bands),
        in_specs=[smem] + [vmem] * 5 + [smem] * 3 + [vmem] * 4,
        out_specs=[vmem, vmem],
        out_shape=[
            jax.ShapeDtypeStruct((local_k, bands, LANES), jnp.float32),
            jax.ShapeDtypeStruct((bands, LANES), jnp.float32),
        ],
        scratch_shapes=[
            pltpu.VMEM((area, depth), jnp.bfloat16),
            pltpu.VMEM((2, area, LANES), jnp.float32),
            pltpu.VMEM((2, area, LANES), jnp.float32),
            pltpu.VMEM((2, area, LANES), jnp.float32),
            pltpu.VMEM((2, area, LANES), jnp.float32),
        ],
        compiler_params=pltpu.CompilerParams(vmem_limit_bytes=VMEM_LIMIT),
        name="pairs",
    )(order, g, weights, early, right, left, e_here, up_here, mask_here, shift, gain, occ, keep)


def greet(axes):
    barrier = pltpu.get_barrier_semaphore()
    for axis, size in axes:
        for hop in range(1, size):
            peer = lax.rem(lax.axis_index(axis) + hop, size)
            pl.semaphore_signal(barrier, inc=1, device_id={axis: peer}, device_id_type=pl.DeviceIdType.MESH)
    pl.semaphore_wait(barrier, sum(size - 1 for _, size in axes))


def send_all(axis, size, source, slots, sends, receives, first):
    me = lax.axis_index(axis)
    copies = []
    for hop in range(1, size):
        copy = pltpu.make_async_remote_copy(
            src_ref=source,
            dst_ref=slots.at[me],
            send_sem=sends.at[first + hop - 1],
            recv_sem=receives.at[first + hop - 1],
            device_id={axis: lax.rem(me + hop, size)},
            device_id_type=pl.DeviceIdType.MESH,
        )
        copy.start()
        copies.append(copy)
    slots[me] = source[...]
    return copies


def sum_kernel(
    sizes, scales, self_ref, mask_ref, width_ref, self_out, width_out,
    self_mine, width_mine, self_slots, width_slots, sends, receives
):
    self_mine[...] = jnp.sum(self_ref[...], 2) * mask_ref[...] * scales[0]
    width = jnp.sum(width_ref[...], 0, keepdims=True) * scales[1]
    width_mine[...] = jnp.broadcast_to(width, width_mine.shape)
    greet((("pb", sizes[0]), ("ka", sizes[1])))
    copies = send_all("pb", sizes[0], self_mine, self_slots, sends, receives, 0)
    copies += send_all("ka", sizes[1], width_mine, width_slots, sends, receives, sizes[0] - 1)
    for copy in copies:
        copy.wait()
    for size, slots, out in ((sizes[0], self_slots, self_out), (sizes[1], width_slots, width_out)):
        total = slots[0]
        for s in range(1, size):
            total += slots[s]
        out[...] = total[: out.shape[0], : out.shape[1]]


def both_sums(self_lanes, mask_here, width_lanes, modes, scales):
    sizes = (lax.axis_size("pb"), lax.axis_size("ka"))
    copies = sizes[0] + sizes[1] - 2
    return pl.pallas_call(
        functools.partial(sum_kernel, sizes, scales),
        in_specs=[pl.BlockSpec(memory_space=pltpu.VMEM)] * 3,
        out_specs=[pl.BlockSpec(memory_space=pltpu.VMEM)] * 2,
        out_shape=[
            jax.ShapeDtypeStruct(mask_here.shape, jnp.float32),
            jax.ShapeDtypeStruct((1, modes), jnp.float32),
        ],
        scratch_shapes=[
            pltpu.VMEM(mask_here.shape, jnp.float32),
            pltpu.VMEM((8, LANES), jnp.float32),
            pltpu.VMEM((sizes[0],) + mask_here.shape, jnp.float32),
            pltpu.VMEM((sizes[1], 8, LANES), jnp.float32),
            pltpu.SemaphoreType.DMA((copies,)),
            pltpu.SemaphoreType.DMA((copies,)),
        ],
        compiler_params=pltpu.CompilerParams(collective_id=0, has_side_effects=True),
        name="sums",
    )(self_lanes, mask_here, width_lanes)


def rows_kernel(sizes, mine_ref, out_ref, ka_slots, pb_slots, sends, receives):
    greet((("ka", sizes[1]), ("pb", sizes[0])))
    for copy in send_all("ka", sizes[1], mine_ref, ka_slots, sends, receives, 0):
        copy.wait()
    for copy in send_all("pb", sizes[0], ka_slots, pb_slots, sends, receives, sizes[1] - 1):
        copy.wait()
    rows, columns = mine_ref.shape
    for source in range(sizes[0]):
        for owner in range(sizes[1]):
            place = slice(owner * rows, (owner + 1) * rows), slice(source * columns, (source + 1) * columns)
            out_ref[place] = pb_slots[source, owner]


def gather_rows(packed):
    sizes = (lax.axis_size("pb"), lax.axis_size("ka"))
    rows, width = packed.shape
    columns = -(-width // (sizes[0] * LANES)) * LANES
    packed = jnp.pad(packed, ((0, 0), (0, columns * sizes[0] - width)))
    mine = lax.dynamic_slice_in_dim(packed, lax.axis_index("pb") * columns, columns, 1)
    copies = sizes[0] + sizes[1] - 2
    return pl.pallas_call(
        functools.partial(rows_kernel, sizes),
        in_specs=[pl.BlockSpec(memory_space=pltpu.VMEM)],
        out_specs=pl.BlockSpec(memory_space=pltpu.VMEM),
        out_shape=jax.ShapeDtypeStruct((sizes[1] * rows, sizes[0] * columns), packed.dtype),
        scratch_shapes=[
            pltpu.VMEM((sizes[1], rows, columns), packed.dtype),
            pltpu.VMEM((sizes[0], sizes[1], rows, columns), packed.dtype),
            pltpu.SemaphoreType.DMA((copies,)),
            pltpu.SemaphoreType.DMA((copies,)),
        ],
        compiler_params=pltpu.CompilerParams(collective_id=1, has_side_effects=True),
        name="rows",
    )(mine)


def lanes_of(first, second):
    pad = [(0, 0)] * (first.ndim - 1) + [(0, HALF - first.shape[-1])]
    return jnp.concatenate([jnp.pad(first, pad), jnp.pad(second, pad)], -1)


def weights_of(phases, mode_pair, pairs):
    _, local_k, vectors = phases.shape
    modes = mode_pair.shape[1]
    wave = phases.astype(jnp.float32)
    vec = mode_pair.astype(jnp.float32).reshape(2, modes // 2 // pairs, pairs, 2, modes)
    vec = jnp.transpose(vec, (0, 1, 3, 2, 4))[..., None, None, :]
    cos, sin = (jnp.transpose(w)[None, None, None, :, :, None] for w in (wave[0], wave[1]))
    real = cos * vec[0] - sin * vec[1]
    imag = cos * vec[1] + sin * vec[0]
    both = jnp.stack([lanes_of(real, imag), lanes_of(-imag, real)]).astype(jnp.bfloat16)
    both = both.reshape(modes // pairs, 2, pairs * vectors, local_k * LANES)
    both = jnp.pad(both, ((0, 0), (0, 0), (0, LANES - pairs * vectors), (0, 0)))
    return both.reshape(modes // pairs, 2 * LANES, local_k * LANES)


def ring_step(array, axis):
    size = lax.axis_size(axis)
    return lax.ppermute(array, axis, [(i, (i + 1) % size) for i in range(size)])


def shards(
    kpoint_coords,
    g_wannier,
    mode_vectors,
    frequencies,
    rotations,
    energies,
    band_window,
    target_owner,
    target_row,
):
    local_k = rotations.shape[0]
    bands = energies.shape[1]
    modes = frequencies.shape[1]
    vectors = g_wannier.shape[1]
    ka_size, pb_size = lax.axis_size("ka"), lax.axis_size("pb")
    ka = lax.axis_index("ka")
    total_k = local_k * ka_size
    area = bands * bands
    pairs = max(n for n in range(1, LANES // vectors + 1) if modes // 2 % n == 0)
    count = modes // pairs
    mask_here = window_mask(band_window, bands)
    packed = jnp.concatenate([rotations, energies, mask_here.astype(jnp.bfloat16)], 1)
    if ka_size == count:
        parts = [g_wannier[0], ring_step(g_wannier[0], "ka")]
        packed, second = lax.optimization_barrier((packed, parts[1]))
        gathered, parts[1] = lax.optimization_barrier((gather_rows(packed), second))
        while len(parts) < count:
            parts.append(ring_step(parts[-1], "ka"))
        order = (ka - jnp.arange(count, dtype=jnp.int32)) % count
    else:
        gathered = gather_rows(packed)
        whole = lax.all_gather(g_wannier, "ka", axis=2, tiled=True)[0]
        parts = jnp.split(whole, count, 1)
        order = jnp.arange(count, dtype=jnp.int32)
    wanted = target_owner[0, :, 0] * local_k + target_row[0]
    choose = (wanted[:, None] == jnp.arange(total_k, dtype=jnp.int32)[None, :]).astype(jnp.bfloat16)
    fetched = jnp.dot(choose, gathered, preferred_element_type=jnp.float32)
    size = 2 * area
    rot_there = fetched[:, :size].astype(jnp.bfloat16).reshape(local_k, 2, bands, bands)
    e_there = fetched[:, size : size + bands]
    mask_there = fetched[:, size + bands : size + 2 * bands]

    weights = weights_of(
        phases_of(kpoint_coords, vectors).reshape(2, local_k, vectors), mode_vectors[0], pairs
    )
    early = early_sums(order, parts[:-1], weights, area)
    rot_here = rotations.reshape(local_k, 2, bands, bands)
    right = jnp.transpose(rot_here, (0, 3, 1, 2)).reshape(local_k, bands, 2 * bands)
    left = jnp.stack([rot_there[:, 0], -rot_there[:, 1]], 1)
    left = jnp.transpose(left, (0, 3, 1, 2)).reshape(local_k, bands, 2 * bands)

    e_here = energies.astype(jnp.float32)
    occ_here = occupation(e_here)
    occ_there = jnp.broadcast_to(occupation(e_there)[:, :, None], (local_k, bands, LANES))
    keep = jnp.broadcast_to(mask_there[:, :, None], (local_k, bands, LANES))
    frequency = frequencies[0]
    bose = 1.0 / (jnp.exp(frequency / THERMAL_KELVIN) - 1.0)
    ones = jnp.ones_like(bose)
    shift = lanes_of(frequency, -frequency)[None, None, :] - e_there[:, :, None]
    gain = keep * (lanes_of(bose, bose + 1.0) + lanes_of(ones, -ones) * occ_there)
    self_lanes, width_lanes = pair_sums(
        order, parts[-1], weights, early, right, left, e_here, occ_here * mask_here, mask_here,
        shift, gain, occ_there, keep, bands,
    )
    scale = SMEARING_WIDTH / math.pi
    scales = (scale / pb_size, 2.0 * math.pi / total_k * scale)
    return both_sums(self_lanes, mask_here, width_lanes, modes, scales)


def solution(mesh):
    in_specs = (
        P(None, ("grp", "ka")),
        P(("grp", "pb"), None, "ka"),
        P(("grp", "pb"), None, None, None),
        P(("grp", "pb"), None),
        P(("grp", "ka"), None),
        P(("grp", "ka"), None),
        P(None, ("grp", "ka")),
        P(("grp", "pb"), "ka", None),
        P(("grp", "pb"), "ka"),
    )
    out_specs = (P(("grp", "ka"), None), P(("grp", "pb"), None))
    return jax.shard_map(shards, mesh=mesh, in_specs=in_specs, out_specs=out_specs, check_vma=False)
```

```python
import functools
import math

import jax
import jax.numpy as jnp
from jax import lax
from jax.experimental import pallas as pl
from jax.experimental.pallas import tpu as pltpu
from jax.sharding import PartitionSpec as P

THERMAL_KELVIN = 0.1
SMEARING_WIDTH = 0.05
LANES = 128
HALF = 64
VMEM_LIMIT = 32 * 1024 * 1024


def window_mask(band_window, bands):
    energy_levels = jnp.arange(bands, dtype=jnp.int32)
    inside = (energy_levels[None, :] >= band_window[0][:, None]) & (
        energy_levels[None, :] < band_window[1][:, None]
    )
    return inside.astype(jnp.float32)


def phases_of(coords, vectors):
    index = jnp.arange(vectors, dtype=jnp.int32)
    first = (index % 2).astype(jnp.float32)
    second = (index // 2 % 2).astype(jnp.float32)
    third = (index // 4 % 2).astype(jnp.float32)
    angle = coords[0][:, None] * first[None, :] + coords[1][:, None] * second[None, :]
    angle = 2.0 * math.pi * (angle + coords[2][:, None] * third[None, :])
    return jnp.concatenate([jnp.cos(angle), jnp.sin(angle)], 0).astype(jnp.bfloat16)


def occupation(energy_value):
    return 1.0 / (1.0 + jnp.exp(energy_value / THERMAL_KELVIN))


def turn_part(g_ref, turned, area):
    vectors, length = g_ref.shape
    pairs = length // (2 * area)
    fill = jnp.zeros((LANES - pairs * vectors, LANES), jnp.float32)

    def tile_of(start):
        rows = [
            g_ref[:, pl.ds(pl.multiple_of(p * 2 * area + start, LANES), LANES)].astype(jnp.float32)
            for p in range(pairs)
        ]
        return jnp.concatenate(rows + [fill], 0).T.astype(jnp.bfloat16)

    whole = area // LANES
    rest = area - whole * LANES

    def even(j, carry):
        spot = pl.multiple_of(j * LANES, LANES)
        turned[pl.ds(spot, LANES), :LANES] = tile_of(spot)
        return carry

    def odd(j, carry):
        spot = pl.multiple_of(j * LANES, LANES)
        turned[pl.ds(pl.multiple_of(spot + LANES - rest, rest), LANES), LANES:] = tile_of(spot + (whole + 1) * LANES)
        return carry

    lax.fori_loop(0, whole, even, 0)
    middle = tile_of(whole * LANES)
    turned[whole * LANES : area, :LANES] = middle[:rest]
    turned[: LANES - rest, LANES:] = middle[rest:]
    lax.fori_loop(0, whole, odd, 0)


def early_kernel(*refs, area):
    order_ref, parts, w_ref, out_ref, turned = refs[0], refs[1:-3], refs[-3], refs[-2], refs[-1]
    for s, g_ref in enumerate(parts):
        turn_part(g_ref, turned.at[s], area)
    chunk = area // 5

    def one_step(step, carry):
        columns = pl.ds(pl.multiple_of(step * 2 * LANES, 2 * LANES), 2 * LANES)
        weights = [w_ref[order_ref[s], :, columns] for s in range(len(parts))]
        for c in range(5):
            rows = slice(c * chunk, (c + 1) * chunk)
            total = 0.0
            for s in range(len(parts)):
                total += jnp.dot(turned[s, rows, :], weights[s], preferred_element_type=jnp.float32)
            out_ref[step, rows, :] = total.astype(out_ref.dtype)
        return carry

    lax.fori_loop(0, out_ref.shape[0], one_step, 0)


def early_sums(order, parts, weights, area):
    count, depth, width = weights.shape
    return pl.pallas_call(
        functools.partial(early_kernel, area=area),
        in_specs=[pl.BlockSpec(memory_space=pltpu.SMEM)]
        + [pl.BlockSpec(memory_space=pltpu.VMEM)] * (len(parts) + 1),
        out_specs=pl.BlockSpec(memory_space=pltpu.VMEM),
        out_shape=jax.ShapeDtypeStruct((width // (2 * LANES), area, 2 * LANES), jnp.bfloat16),
        scratch_shapes=[pltpu.VMEM((len(parts), area, depth), jnp.bfloat16)],
        compiler_params=pltpu.CompilerParams(vmem_limit_bytes=VMEM_LIMIT),
        cost_estimate=pl.CostEstimate(
            flops=2 * len(parts) * area * depth * width,
            bytes_accessed=2 * area * width + 2 * weights.size,
            transcendentals=0,
        ),
        name="early",
    )(order, *parts, weights)


def pair_kernel(
    order_ref, g_ref, w_ref, early_ref, right_ref, left_ref, e_ref, up_ref, mask_ref,
    shift_ref, gain_ref, occ_ref, keep_ref, self_ref, width_ref, turned, modal, half, *, bands
):
    area = bands * bands
    width_ref[...] = jnp.zeros_like(width_ref)
    turn_part(g_ref, turned, area)
    chunk = 8 * bands
    lane = lax.broadcasted_iota(jnp.int32, (bands, LANES), 1)
    sign = jnp.where(lane < HALF, -1.0, 1.0)

    def operand(block):
        block = jnp.concatenate([block, pltpu.roll(block, HALF, 1) * sign], 0)
        return block.astype(jnp.bfloat16)

    def one_k(kk, step):
        k = step * 2 + kk
        right = right_ref[k]
        for a in range(0, bands, 2):
            pair = [operand(modal[kk, (a + s) * bands : (a + s + 1) * bands, :]) for s in range(2)]
            out = jnp.dot(right, jnp.concatenate(pair, 1), preferred_element_type=jnp.float32)
            for s in range(2):
                half[pl.ds(a + s, bands, stride=bands), :] = out[:, s * LANES : (s + 1) * LANES]
        left = left_ref[k]
        shift = shift_ref[k]
        gain = gain_ref[k]
        occ = occ_ref[k]
        total = jnp.zeros((bands, LANES), jnp.float32)
        for n in range(0, bands, 2):
            pair = [operand(half[(n + s) * bands : (n + s + 1) * bands, :]) for s in range(2)]
            out = jnp.dot(left, jnp.concatenate(pair, 1), preferred_element_type=jnp.float32)
            for s in range(2):
                coupling = out[:, s * LANES : (s + 1) * LANES]
                square = coupling * coupling
                strength = square + pltpu.roll(square, HALF, 1)
                x = shift + e_ref[k, n + s]
                term = strength / (x * x + SMEARING_WIDTH * SMEARING_WIDTH)
                self_ref[k, n + s : n + s + 1, :] = jnp.sum(term * gain, 0, keepdims=True)
                total += term * (up_ref[k, n + s] - mask_ref[k, n + s] * occ)
        width_ref[...] += total * keep_ref[k]
        return step

    def one_step(step, carry):
        columns = pl.ds(pl.multiple_of(step * 2 * LANES, 2 * LANES), 2 * LANES)
        weight = w_ref[order_ref[w_ref.shape[0] - 1], :, columns]
        for c in range(area // chunk):
            rows = slice(c * chunk, (c + 1) * chunk)
            both = early_ref[step, rows, :].astype(jnp.float32) + jnp.dot(
                turned[rows, :], weight, preferred_element_type=jnp.float32
            )
            for kk in range(2):
                modal[kk, rows, :] = both[:, kk * LANES : (kk + 1) * LANES]
        lax.fori_loop(0, 2, one_k, step)
        return carry

    lax.fori_loop(0, right_ref.shape[0] // 2, one_step, 0)


def pair_sums(order, g, weights, early, right, left, e_here, up_here, mask_here, shift, gain, occ, keep, bands):
    local_k = right.shape[0]
    depth = weights.shape[1]
    area = bands * bands
    vmem = pl.BlockSpec(memory_space=pltpu.VMEM)
    smem = pl.BlockSpec(memory_space=pltpu.SMEM)
    return pl.pallas_call(
        functools.partial(pair_kernel, bands=bands),
        in_specs=[smem] + [vmem] * 5 + [smem] * 3 + [vmem] * 4,
        out_specs=[vmem, vmem],
        out_shape=[
            jax.ShapeDtypeStruct((local_k, bands, LANES), jnp.float32),
            jax.ShapeDtypeStruct((bands, LANES), jnp.float32),
        ],
        scratch_shapes=[
            pltpu.VMEM((area, depth), jnp.bfloat16),
            pltpu.VMEM((2, area, LANES), jnp.float32),
            pltpu.VMEM((area, LANES), jnp.float32),
        ],
        compiler_params=pltpu.CompilerParams(vmem_limit_bytes=VMEM_LIMIT),
        name="pairs",
    )(order, g, weights, early, right, left, e_here, up_here, mask_here, shift, gain, occ, keep)


def greet(axes):
    barrier = pltpu.get_barrier_semaphore()
    for axis, size in axes:
        for hop in range(1, size):
            peer = lax.rem(lax.axis_index(axis) + hop, size)
            pl.semaphore_signal(barrier, inc=1, device_id={axis: peer}, device_id_type=pl.DeviceIdType.MESH)
    pl.semaphore_wait(barrier, sum(size - 1 for _, size in axes))


def send_all(axis, size, source, slots, sends, receives, first):
    me = lax.axis_index(axis)
    copies = []
    for hop in range(1, size):
        copy = pltpu.make_async_remote_copy(
            src_ref=source,
            dst_ref=slots.at[me],
            send_sem=sends.at[first + hop - 1],
            recv_sem=receives.at[first + hop - 1],
            device_id={axis: lax.rem(me + hop, size)},
            device_id_type=pl.DeviceIdType.MESH,
        )
        copy.start()
        copies.append(copy)
    slots[me] = source[...]
    return copies


def sum_kernel(
    sizes, scales, self_ref, mask_ref, width_ref, self_out, width_out,
    self_mine, width_mine, self_slots, width_slots, sends, receives
):
    self_mine[...] = jnp.sum(self_ref[...], 2) * mask_ref[...] * scales[0]
    width = jnp.sum(width_ref[...], 0, keepdims=True) * scales[1]
    width_mine[...] = jnp.broadcast_to(width, width_mine.shape)
    greet((("pb", sizes[0]), ("ka", sizes[1])))
    copies = send_all("pb", sizes[0], self_mine, self_slots, sends, receives, 0)
    copies += send_all("ka", sizes[1], width_mine, width_slots, sends, receives, sizes[0] - 1)
    for copy in copies:
        copy.wait()
    for size, slots, out in ((sizes[0], self_slots, self_out), (sizes[1], width_slots, width_out)):
        total = slots[0]
        for s in range(1, size):
            total += slots[s]
        out[...] = total[: out.shape[0], : out.shape[1]]


def both_sums(self_lanes, mask_here, width_lanes, modes, scales):
    sizes = (lax.axis_size("pb"), lax.axis_size("ka"))
    copies = sizes[0] + sizes[1] - 2
    return pl.pallas_call(
        functools.partial(sum_kernel, sizes, scales),
        in_specs=[pl.BlockSpec(memory_space=pltpu.VMEM)] * 3,
        out_specs=[pl.BlockSpec(memory_space=pltpu.VMEM)] * 2,
        out_shape=[
            jax.ShapeDtypeStruct(mask_here.shape, jnp.float32),
            jax.ShapeDtypeStruct((1, modes), jnp.float32),
        ],
        scratch_shapes=[
            pltpu.VMEM(mask_here.shape, jnp.float32),
            pltpu.VMEM((8, LANES), jnp.float32),
            pltpu.VMEM((sizes[0],) + mask_here.shape, jnp.float32),
            pltpu.VMEM((sizes[1], 8, LANES), jnp.float32),
            pltpu.SemaphoreType.DMA((copies,)),
            pltpu.SemaphoreType.DMA((copies,)),
        ],
        compiler_params=pltpu.CompilerParams(collective_id=0, has_side_effects=True),
        name="sums",
    )(self_lanes, mask_here, width_lanes)


def lanes_of(first, second):
    pad = [(0, 0)] * (first.ndim - 1) + [(0, HALF - first.shape[-1])]
    return jnp.concatenate([jnp.pad(first, pad), jnp.pad(second, pad)], -1)


def weights_of(phases, mode_pair, pairs, behind):
    _, local_k, vectors = phases.shape
    modes = mode_pair.shape[1]
    wave = phases.astype(jnp.float32)
    vec = mode_pair.astype(jnp.float32).reshape(2, modes // 2 // pairs, pairs, 2, modes)
    vec = jnp.transpose(vec, (0, 1, 3, 2, 4))[..., None, None, :]
    cos, sin = (jnp.transpose(w)[None, None, None, :, :, None] for w in (wave[0], wave[1]))
    real = (cos * vec[0] - sin * vec[1]).astype(jnp.bfloat16)
    imag = (cos * vec[1] + sin * vec[0]).astype(jnp.bfloat16)
    real, imag, behind = lax.optimization_barrier((real, imag, behind))
    both = jnp.stack([lanes_of(real, imag), lanes_of(-imag, real)])
    both = both.reshape(modes // pairs, 2, pairs * vectors, local_k * LANES)
    both = jnp.pad(both, ((0, 0), (0, 0), (0, LANES - pairs * vectors), (0, 0)))
    return both.reshape(modes // pairs, 2 * LANES, local_k * LANES), behind


def ring_step(array, axis):
    size = lax.axis_size(axis)
    return lax.ppermute(array, axis, [(i, (i + 1) % size) for i in range(size)])


def from_each(array, axis):
    size = lax.axis_size(axis)
    return [array] + [
        lax.ppermute(array, axis, [(i, (i + hop) % size) for i in range(size)]) for hop in range(1, size)
    ]


def shards(
    kpoint_coords,
    g_wannier,
    mode_vectors,
    frequencies,
    rotations,
    energies,
    band_window,
    target_owner,
    target_row,
):
    local_k = rotations.shape[0]
    bands = energies.shape[1]
    modes = frequencies.shape[1]
    vectors = g_wannier.shape[1]
    ka_size, pb_size = lax.axis_size("ka"), lax.axis_size("pb")
    ka, pb = lax.axis_index("ka"), lax.axis_index("pb")
    total_k = local_k * ka_size
    area = bands * bands
    pairs = max(n for n in range(1, LANES // vectors + 1) if modes // 2 % n == 0)
    count = modes // pairs
    mask_here = window_mask(band_window, bands)
    packed = jnp.concatenate([rotations, energies, mask_here.astype(jnp.bfloat16)], 1)
    share = local_k // 2
    mine = lax.dynamic_slice_in_dim(packed, pb % 2 * share, share, 0)
    mine = jnp.concatenate(from_each(mine, "ka"), 0)
    other = lax.ppermute(mine, "pb", [(i, i ^ 1) for i in range(pb_size)])
    gathered = jnp.concatenate([mine, other], 0)
    phases = phases_of(kpoint_coords, vectors).reshape(2, local_k, vectors)
    if ka_size == count:
        parts = [g_wannier[0], ring_step(g_wannier[0], "ka")]
        order = (ka - jnp.arange(count, dtype=jnp.int32)) % count
    else:
        whole = lax.all_gather(g_wannier, "ka", axis=2, tiled=True)[0]
        parts = jnp.split(whole, count, 1)
        order = jnp.arange(count, dtype=jnp.int32)
    weights, parts[1] = weights_of(phases, mode_vectors[0], pairs, parts[1])
    while len(parts) < count:
        parts.append(ring_step(parts[-1], "ka"))
    owner, row = target_owner[0, :, 0], target_row[0]
    wanted = ((pb - row // share) % 2 * ka_size + (ka - owner) % ka_size) * share + row % share
    choose = (wanted[:, None] == jnp.arange(total_k, dtype=jnp.int32)[None, :]).astype(jnp.bfloat16)
    fetched = jnp.dot(choose, gathered, preferred_element_type=jnp.float32)
    size = 2 * area
    rot_there = fetched[:, :size].astype(jnp.bfloat16).reshape(local_k, 2, bands, bands)
    e_there = fetched[:, size : size + bands]
    mask_there = fetched[:, size + bands : size + 2 * bands]

    early = early_sums(order, parts[:-1], weights, area)
    rot_here = rotations.reshape(local_k, 2, bands, bands)
    right = jnp.transpose(rot_here, (0, 3, 1, 2)).reshape(local_k, bands, 2 * bands)
    left = jnp.stack([rot_there[:, 0], -rot_there[:, 1]], 1)
    left = jnp.transpose(left, (0, 3, 1, 2)).reshape(local_k, bands, 2 * bands)

    e_here = energies.astype(jnp.float32)
    occ_here = occupation(e_here)
    occ_there = jnp.broadcast_to(occupation(e_there)[:, :, None], (local_k, bands, LANES))
    keep = jnp.broadcast_to(mask_there[:, :, None], (local_k, bands, LANES))
    frequency = frequencies[0]
    bose = 1.0 / (jnp.exp(frequency / THERMAL_KELVIN) - 1.0)
    ones = jnp.ones_like(bose)
    shift = lanes_of(frequency, -frequency)[None, None, :] - e_there[:, :, None]
    gain = keep * (lanes_of(bose, bose + 1.0) + lanes_of(ones, -ones) * occ_there)
    self_lanes, width_lanes = pair_sums(
        order, parts[-1], weights, early, right, left, e_here, occ_here * mask_here, mask_here,
        shift, gain, occ_there, keep, bands,
    )
    scale = SMEARING_WIDTH / math.pi
    scales = (scale / pb_size, 2.0 * math.pi / total_k * scale)
    return both_sums(self_lanes, mask_here, width_lanes, modes, scales)


def solution(mesh):
    in_specs = (
        P(None, ("grp", "ka")),
        P(("grp", "pb"), None, "ka"),
        P(("grp", "pb"), None, None, None),
        P(("grp", "pb"), None),
        P(("grp", "ka"), None),
        P(("grp", "ka"), None),
        P(None, ("grp", "ka")),
        P(("grp", "pb"), "ka", None),
        P(("grp", "pb"), "ka"),
    )
    out_specs = (P(("grp", "ka"), None), P(("grp", "pb"), None))
    return jax.shard_map(shards, mesh=mesh, in_specs=in_specs, out_specs=out_specs, check_vma=False)
```

```python
import functools
import math

import jax
import jax.numpy as jnp
from jax import lax
from jax.experimental import pallas as pl
from jax.experimental.pallas import tpu as pltpu
from jax.sharding import PartitionSpec as P

THERMAL_KELVIN = 0.1
SMEARING_WIDTH = 0.05
LANES = 128
HALF = 64
VMEM_LIMIT = 32 * 1024 * 1024


def window_mask(band_window, bands):
    energy_levels = jnp.arange(bands, dtype=jnp.int32)
    inside = (energy_levels[None, :] >= band_window[0][:, None]) & (
        energy_levels[None, :] < band_window[1][:, None]
    )
    return inside.astype(jnp.float32)


def phases_of(coords, vectors):
    index = jnp.arange(vectors, dtype=jnp.int32)
    first = (index % 2).astype(jnp.float32)
    second = (index // 2 % 2).astype(jnp.float32)
    third = (index // 4 % 2).astype(jnp.float32)
    angle = coords[0][:, None] * first[None, :] + coords[1][:, None] * second[None, :]
    angle = 2.0 * math.pi * (angle + coords[2][:, None] * third[None, :])
    return jnp.concatenate([jnp.cos(angle), jnp.sin(angle)], 0).astype(jnp.bfloat16)


def occupation(energy_value):
    return 1.0 / (1.0 + jnp.exp(energy_value / THERMAL_KELVIN))


def turn_part(g_ref, turned, area):
    vectors, length = g_ref.shape
    pairs = length // (2 * area)
    fill = jnp.zeros((LANES - pairs * vectors, LANES), jnp.float32)

    def tile_of(start):
        rows = [
            g_ref[:, pl.ds(pl.multiple_of(p * 2 * area + start, LANES), LANES)].astype(jnp.float32)
            for p in range(pairs)
        ]
        return jnp.concatenate(rows + [fill], 0).T.astype(jnp.bfloat16)

    whole = area // LANES
    rest = area - whole * LANES

    def even(j, carry):
        spot = pl.multiple_of(j * LANES, LANES)
        turned[pl.ds(spot, LANES), :LANES] = tile_of(spot)
        return carry

    def odd(j, carry):
        spot = pl.multiple_of(j * LANES, LANES)
        turned[pl.ds(pl.multiple_of(spot + LANES - rest, rest), LANES), LANES:] = tile_of(spot + (whole + 1) * LANES)
        return carry

    lax.fori_loop(0, whole, even, 0)
    middle = tile_of(whole * LANES)
    turned[whole * LANES : area, :LANES] = middle[:rest]
    turned[: LANES - rest, LANES:] = middle[rest:]
    lax.fori_loop(0, whole, odd, 0)


def early_kernel(*refs, area):
    order_ref, parts, w_ref, out_ref, turned = refs[0], refs[1:-3], refs[-3], refs[-2], refs[-1]
    for s, g_ref in enumerate(parts):
        turn_part(g_ref, turned.at[s], area)
    chunk = area // 5

    def one_step(step, carry):
        columns = pl.ds(pl.multiple_of(step * 2 * LANES, 2 * LANES), 2 * LANES)
        weights = [w_ref[order_ref[s], :, columns] for s in range(len(parts))]
        for c in range(5):
            rows = slice(c * chunk, (c + 1) * chunk)
            total = 0.0
            for s in range(len(parts)):
                total += jnp.dot(turned[s, rows, :], weights[s], preferred_element_type=jnp.float32)
            out_ref[step, rows, :] = total.astype(out_ref.dtype)
        return carry

    lax.fori_loop(0, out_ref.shape[0], one_step, 0)


def early_sums(order, parts, weights, area):
    count, depth, width = weights.shape
    return pl.pallas_call(
        functools.partial(early_kernel, area=area),
        in_specs=[pl.BlockSpec(memory_space=pltpu.SMEM)]
        + [pl.BlockSpec(memory_space=pltpu.VMEM)] * (len(parts) + 1),
        out_specs=pl.BlockSpec(memory_space=pltpu.VMEM),
        out_shape=jax.ShapeDtypeStruct((width // (2 * LANES), area, 2 * LANES), jnp.bfloat16),
        scratch_shapes=[pltpu.VMEM((len(parts), area, depth), jnp.bfloat16)],
        compiler_params=pltpu.CompilerParams(vmem_limit_bytes=VMEM_LIMIT),
        cost_estimate=pl.CostEstimate(
            flops=2 * len(parts) * area * depth * width,
            bytes_accessed=2 * area * width + 2 * weights.size,
            transcendentals=0,
        ),
        name="early",
    )(order, *parts, weights)


def pair_kernel(
    order_ref, g_ref, w_ref, early_ref, right_ref, left_ref, e_ref, up_ref, mask_ref,
    shift_ref, gain_ref, occ_ref, keep_ref, self_ref, width_ref, turned, modal, half, *, bands
):
    area = bands * bands
    width_ref[...] = jnp.zeros_like(width_ref)
    turn_part(g_ref, turned, area)
    chunk = 8 * bands
    lane = lax.broadcasted_iota(jnp.int32, (bands, LANES), 1)
    sign = jnp.where(lane < HALF, -1.0, 1.0)

    def operand(block):
        block = jnp.concatenate([block, pltpu.roll(block, HALF, 1) * sign], 0)
        return block.astype(jnp.bfloat16)

    def one_k(kk, step):
        k = step * 2 + kk
        right = right_ref[k]
        for a in range(0, bands, 2):
            pair = [operand(modal[kk, (a + s) * bands : (a + s + 1) * bands, :]) for s in range(2)]
            out = jnp.dot(right, jnp.concatenate(pair, 1), preferred_element_type=jnp.float32)
            for s in range(2):
                half[pl.ds(a + s, bands, stride=bands), :] = out[:, s * LANES : (s + 1) * LANES]
        left = left_ref[k]
        shift = shift_ref[k]
        gain = gain_ref[k]
        occ = occ_ref[k]
        total = jnp.zeros((bands, LANES), jnp.float32)
        for n in range(0, bands, 2):
            pair = [operand(half[(n + s) * bands : (n + s + 1) * bands, :]) for s in range(2)]
            out = jnp.dot(left, jnp.concatenate(pair, 1), preferred_element_type=jnp.float32)
            for s in range(2):
                coupling = out[:, s * LANES : (s + 1) * LANES]
                square = coupling * coupling
                strength = square + pltpu.roll(square, HALF, 1)
                x = shift + e_ref[k, n + s]
                term = strength / (x * x + SMEARING_WIDTH * SMEARING_WIDTH)
                self_ref[k, n + s : n + s + 1, :] = jnp.sum(term * gain, 0, keepdims=True)
                total += term * (up_ref[k, n + s] - mask_ref[k, n + s] * occ)
        width_ref[...] += total * keep_ref[k]
        return step

    def one_step(step, carry):
        columns = pl.ds(pl.multiple_of(step * 2 * LANES, 2 * LANES), 2 * LANES)
        weight = w_ref[order_ref[w_ref.shape[0] - 1], :, columns]
        for c in range(area // chunk):
            rows = slice(c * chunk, (c + 1) * chunk)
            both = early_ref[step, rows, :].astype(jnp.float32) + jnp.dot(
                turned[rows, :], weight, preferred_element_type=jnp.float32
            )
            for kk in range(2):
                modal[kk, rows, :] = both[:, kk * LANES : (kk + 1) * LANES]
        lax.fori_loop(0, 2, one_k, step)
        return carry

    lax.fori_loop(0, right_ref.shape[0] // 2, one_step, 0)


def pair_sums(order, g, weights, early, right, left, e_here, up_here, mask_here, shift, gain, occ, keep, bands):
    local_k = right.shape[0]
    depth = weights.shape[1]
    area = bands * bands
    vmem = pl.BlockSpec(memory_space=pltpu.VMEM)
    smem = pl.BlockSpec(memory_space=pltpu.SMEM)
    return pl.pallas_call(
        functools.partial(pair_kernel, bands=bands),
        in_specs=[smem] + [vmem] * 5 + [smem] * 3 + [vmem] * 4,
        out_specs=[vmem, vmem],
        out_shape=[
            jax.ShapeDtypeStruct((local_k, bands, LANES), jnp.float32),
            jax.ShapeDtypeStruct((bands, LANES), jnp.float32),
        ],
        scratch_shapes=[
            pltpu.VMEM((area, depth), jnp.bfloat16),
            pltpu.VMEM((2, area, LANES), jnp.float32),
            pltpu.VMEM((area, LANES), jnp.float32),
        ],
        compiler_params=pltpu.CompilerParams(vmem_limit_bytes=VMEM_LIMIT),
        name="pairs",
    )(order, g, weights, early, right, left, e_here, up_here, mask_here, shift, gain, occ, keep)


def greet(axes):
    barrier = pltpu.get_barrier_semaphore()
    for axis, size in axes:
        for hop in range(1, size):
            peer = lax.rem(lax.axis_index(axis) + hop, size)
            pl.semaphore_signal(barrier, inc=1, device_id={axis: peer}, device_id_type=pl.DeviceIdType.MESH)
    pl.semaphore_wait(barrier, sum(size - 1 for _, size in axes))


def send_all(axis, size, source, slots, sends, receives, first):
    me = lax.axis_index(axis)
    copies = []
    for hop in range(1, size):
        copy = pltpu.make_async_remote_copy(
            src_ref=source,
            dst_ref=slots.at[me],
            send_sem=sends.at[first + hop - 1],
            recv_sem=receives.at[first + hop - 1],
            device_id={axis: lax.rem(me + hop, size)},
            device_id_type=pl.DeviceIdType.MESH,
        )
        copy.start()
        copies.append(copy)
    slots[me] = source[...]
    return copies


def sum_kernel(
    sizes, scales, self_ref, mask_ref, width_ref, self_out, width_out,
    self_mine, width_mine, self_slots, width_slots, sends, receives
):
    self_mine[...] = jnp.sum(self_ref[...], 2) * mask_ref[...] * scales[0]
    width = jnp.sum(width_ref[...], 0, keepdims=True) * scales[1]
    width_mine[...] = jnp.broadcast_to(width, width_mine.shape)
    greet((("pb", sizes[0]), ("ka", sizes[1])))
    copies = send_all("pb", sizes[0], self_mine, self_slots, sends, receives, 0)
    copies += send_all("ka", sizes[1], width_mine, width_slots, sends, receives, sizes[0] - 1)
    for copy in copies:
        copy.wait()
    for size, slots, out in ((sizes[0], self_slots, self_out), (sizes[1], width_slots, width_out)):
        total = slots[0]
        for s in range(1, size):
            total += slots[s]
        out[...] = total[: out.shape[0], : out.shape[1]]


def both_sums(self_lanes, mask_here, width_lanes, modes, scales):
    sizes = (lax.axis_size("pb"), lax.axis_size("ka"))
    copies = sizes[0] + sizes[1] - 2
    return pl.pallas_call(
        functools.partial(sum_kernel, sizes, scales),
        in_specs=[pl.BlockSpec(memory_space=pltpu.VMEM)] * 3,
        out_specs=[pl.BlockSpec(memory_space=pltpu.VMEM)] * 2,
        out_shape=[
            jax.ShapeDtypeStruct(mask_here.shape, jnp.float32),
            jax.ShapeDtypeStruct((1, modes), jnp.float32),
        ],
        scratch_shapes=[
            pltpu.VMEM(mask_here.shape, jnp.float32),
            pltpu.VMEM((8, LANES), jnp.float32),
            pltpu.VMEM((sizes[0],) + mask_here.shape, jnp.float32),
            pltpu.VMEM((sizes[1], 8, LANES), jnp.float32),
            pltpu.SemaphoreType.DMA((copies,)),
            pltpu.SemaphoreType.DMA((copies,)),
        ],
        compiler_params=pltpu.CompilerParams(collective_id=0, has_side_effects=True),
        name="sums",
    )(self_lanes, mask_here, width_lanes)


def lanes_of(first, second):
    pad = [(0, 0)] * (first.ndim - 1) + [(0, HALF - first.shape[-1])]
    return jnp.concatenate([jnp.pad(first, pad), jnp.pad(second, pad)], -1)


def weights_of(phases, mode_pair, pairs, behind):
    _, local_k, vectors = phases.shape
    modes = mode_pair.shape[1]
    wave = phases.astype(jnp.float32)
    vec = mode_pair.astype(jnp.float32).reshape(2, modes // 2 // pairs, pairs, 2, modes)
    vec = jnp.transpose(vec, (0, 1, 3, 2, 4))[..., None, None, :]
    cos, sin = (jnp.transpose(w)[None, None, None, :, :, None] for w in (wave[0], wave[1]))
    real = (cos * vec[0] - sin * vec[1]).astype(jnp.bfloat16)
    imag = (cos * vec[1] + sin * vec[0]).astype(jnp.bfloat16)
    real, imag, behind = lax.optimization_barrier((real, imag, behind))
    both = jnp.stack([lanes_of(real, imag), lanes_of(-imag, real)])
    both = both.reshape(modes // pairs, 2, pairs * vectors, local_k * LANES)
    both = jnp.pad(both, ((0, 0), (0, 0), (0, LANES - pairs * vectors), (0, 0)))
    return both.reshape(modes // pairs, 2 * LANES, local_k * LANES), behind


def ring_step(array, axis):
    size = lax.axis_size(axis)
    return lax.ppermute(array, axis, [(i, (i + 1) % size) for i in range(size)])


def from_each(array, axis):
    size = lax.axis_size(axis)
    return [array] + [
        lax.ppermute(array, axis, [(i, (i + hop) % size) for i in range(size)]) for hop in range(1, size)
    ]


def shards(
    kpoint_coords,
    g_wannier,
    mode_vectors,
    frequencies,
    rotations,
    energies,
    band_window,
    target_owner,
    target_row,
):
    local_k = rotations.shape[0]
    bands = energies.shape[1]
    modes = frequencies.shape[1]
    vectors = g_wannier.shape[1]
    ka_size, pb_size = lax.axis_size("ka"), lax.axis_size("pb")
    ka, pb = lax.axis_index("ka"), lax.axis_index("pb")
    total_k = local_k * ka_size
    area = bands * bands
    pairs = max(n for n in range(1, LANES // vectors + 1) if modes // 2 % n == 0)
    count = modes // pairs
    mask_here = window_mask(band_window, bands)
    packed = jnp.concatenate([rotations, energies, mask_here.astype(jnp.bfloat16)], 1)
    if ka_size == count:
        behind = ring_step(g_wannier[0], "ka")
        packed, behind = lax.optimization_barrier((packed, behind))
    share = local_k // 2
    mine = lax.dynamic_slice_in_dim(packed, pb % 2 * share, share, 0)
    mine = jnp.concatenate(from_each(mine, "ka"), 0)
    other = lax.ppermute(mine, "pb", [(i, i ^ 1) for i in range(pb_size)])
    gathered = jnp.concatenate([mine, other], 0)
    phases = phases_of(kpoint_coords, vectors).reshape(2, local_k, vectors)
    if ka_size == count:
        parts = [g_wannier[0], behind]
        order = (ka - jnp.arange(count, dtype=jnp.int32)) % count
    else:
        whole = lax.all_gather(g_wannier, "ka", axis=2, tiled=True)[0]
        parts = jnp.split(whole, count, 1)
        order = jnp.arange(count, dtype=jnp.int32)
    weights, parts[1] = weights_of(phases, mode_vectors[0], pairs, parts[1])
    while len(parts) < count:
        parts.append(ring_step(parts[-1], "ka"))
    owner, row = target_owner[0, :, 0], target_row[0]
    wanted = ((pb - row // share) % 2 * ka_size + (ka - owner) % ka_size) * share + row % share
    choose = (wanted[:, None] == jnp.arange(total_k, dtype=jnp.int32)[None, :]).astype(jnp.bfloat16)
    fetched = jnp.dot(choose, gathered, preferred_element_type=jnp.float32)
    size = 2 * area
    rot_there = fetched[:, :size].astype(jnp.bfloat16).reshape(local_k, 2, bands, bands)
    e_there = fetched[:, size : size + bands]
    mask_there = fetched[:, size + bands : size + 2 * bands]

    early = early_sums(order, parts[:-1], weights, area)
    rot_here = rotations.reshape(local_k, 2, bands, bands)
    right = jnp.transpose(rot_here, (0, 3, 1, 2)).reshape(local_k, bands, 2 * bands)
    left = jnp.stack([rot_there[:, 0], -rot_there[:, 1]], 1)
    left = jnp.transpose(left, (0, 3, 1, 2)).reshape(local_k, bands, 2 * bands)

    e_here = energies.astype(jnp.float32)
    occ_here = occupation(e_here)
    occ_there = jnp.broadcast_to(occupation(e_there)[:, :, None], (local_k, bands, LANES))
    keep = jnp.broadcast_to(mask_there[:, :, None], (local_k, bands, LANES))
    frequency = frequencies[0]
    bose = 1.0 / (jnp.exp(frequency / THERMAL_KELVIN) - 1.0)
    ones = jnp.ones_like(bose)
    shift = lanes_of(frequency, -frequency)[None, None, :] - e_there[:, :, None]
    gain = keep * (lanes_of(bose, bose + 1.0) + lanes_of(ones, -ones) * occ_there)
    self_lanes, width_lanes = pair_sums(
        order, parts[-1], weights, early, right, left, e_here, occ_here * mask_here, mask_here,
        shift, gain, occ_there, keep, bands,
    )
    scale = SMEARING_WIDTH / math.pi
    scales = (scale / pb_size, 2.0 * math.pi / total_k * scale)
    return both_sums(self_lanes, mask_here, width_lanes, modes, scales)


def solution(mesh):
    in_specs = (
        P(None, ("grp", "ka")),
        P(("grp", "pb"), None, "ka"),
        P(("grp", "pb"), None, None, None),
        P(("grp", "pb"), None),
        P(("grp", "ka"), None),
        P(("grp", "ka"), None),
        P(None, ("grp", "ka")),
        P(("grp", "pb"), "ka", None),
        P(("grp", "pb"), "ka"),
    )
    out_specs = (P(("grp", "ka"), None), P(("grp", "pb"), None))
    return jax.shard_map(shards, mesh=mesh, in_specs=in_specs, out_specs=out_specs, check_vma=False)
```
